32 devices in a mesh: groups: 2 (over y), strip: 4 (over z), angle: 2 (over x), depth: 2 (over core).
Axes of the slice: x: 2, y: 2, z: 4, core: 2. Of those that a mesh axis runs over, the one named last changes fastest.
Arguments:
- crystal: bfloat16 [16, 2, 512, 384], P(('groups', 'depth'), None, 'strip'), parts along dimension 0, may hold values from -4 to 4
- probe: bfloat16 [2, 256, 256], replicated, may hold values from -5 to 5
- amplitude: bfloat16 [4, 2048, 256], P('angle', ('groups', 'strip', 'depth')), parts along dimension 1, may hold values from 0.5 to 8
- shear: int32 [16, 8], P(('groups', 'angle'), 'depth'), parts along dimension 0, may hold values from 0 to 15
- scan_x: int32 [4, 4, 2], P(('groups', 'angle')), parts along dimension 0, may hold values from 0 to 112
- scan_y: int32 [4, 4, 2], P(('groups', 'angle')), parts along dimension 0, may hold values from 0 to 128
- slot_angle: int32 [4, 4, 2], P(('groups', 'angle')), parts along dimension 0, may hold values from 0 to 3
- owner_slot: int32 [4, 4, 2], P(('groups', 'angle')), parts along dimension 0, may hold values from 0 to 1, each once within a row
- counts: int32 [4, 4], P(('groups', 'angle')), parts along dimension 0, may hold values from 1 to 2
Outputs:
- gradient: float32 [16, 2, 512, 384], P(('groups', 'depth'), None, ('strip', 'angle')), parts along dimension 0
The draws below stay inside these ranges and needn't reach their ends.
There are 2 independent parts, one for each index of `groups`. The reference program is written for one: setup_inputs(seed, part) draws one part's arguments, and reference() takes and returns one part's arrays. A program takes and returns all parts, laid end to end along the dimension named above; an argument that names none is the same for every part. Nothing has to cross between parts.
Inputs may be any that keep to these rules, and one draw needn't show every extreme that they name: `owner_slot`: for each angle group and home strip, the 2 entries are a permutation of 0 to 1.
All inputs are finite; a program needn't handle non-finite values.
Results may differ from the reference program's by a relative error of at most 0.02.
Values may be sent and summed in bfloat16 or wider, within the bound.
No kernel may reach another device: no remote copies, remote signals or barrier semaphores. Data moves between devices by JAX's collectives and lax.ppermute only.
A program may use at most 64 MiB of HBM per device.

```python
import math
import jax
import jax.numpy as jnp
from jax import lax

FRAME = 256
WX = 128
SHEAR = 16
NY = 384
NZ_DEV = 4
ANG_DEV = 4
BAND = 144
M = 2
NX = 512
NZ = 8
ANGLES = 8
ANGLE_GROUPS = 2
SLOTS = 4
N_STRIP = 4
N_ANGLE = 2
N_DEPTH = 2


def set_ends(entries, rng, low, largest):
    longest = entries.shape.index(max(entries.shape))
    spots = []
    for shift in (0, 1):
        where = [jax.random.randint(jax.random.fold_in(rng, axis), (), 0, length) for axis, length in enumerate(entries.shape)]
        where[longest] = (where[longest] + shift) % entries.shape[longest]
        spots.append(tuple(where))
    return entries.at[spots[0]].set(low).at[spots[1]].set(largest)


def block_levels(key, dims, shards, smallest, high):
    factor_of = 1.0
    for dim, parts in shards:
        steps = jax.random.uniform(jax.random.fold_in(jax.random.fold_in(key, 6), dim), (parts,), jnp.float32, smallest / len(shards), high / len(shards))
        factor_of = factor_of * jnp.repeat(jnp.exp(steps), dims[dim] // parts).reshape((-1,) + (1,) * (len(dims) - 1 - dim))
    return factor_of


def centred(rng, extent, spread, bound, split=(), held_as=jnp.bfloat16):
    array = spread * jax.random.normal(rng, extent, jnp.float32)
    if split:
        array = array * block_levels(rng, extent, split, -0.22, 0.18)
    return jnp.clip(array, -bound, bound).astype(held_as)


def setup_inputs(seed: int = 0, part: int = 0) -> dict:
    key_of = jax.random.split(jax.random.key(seed), 10)
    part_keys = jax.random.split(jax.random.fold_in(key_of[9], part), 10)
    return {
        "crystal": centred(part_keys[0], (NZ, 2, NX, NY), 0.5, 4.0, ((0, 2), (2, 4))),
        "probe": centred(key_of[1], (2, FRAME, FRAME), 1.0, 5.0),
        "amplitude": jnp.clip(jnp.exp(math.log(8.0) - 2.7725887 * jax.random.uniform(part_keys[2], (SLOTS, N_STRIP * FRAME, FRAME), jnp.float32) ** block_levels(part_keys[2], (SLOTS, N_STRIP * FRAME, FRAME), ((0, 2), (1, 8)), -0.2, 0.2)), 0.5, 8.0).astype(jnp.bfloat16),
        "shear": set_ends(jax.random.randint(part_keys[3], (ANGLES, NZ), 0, SHEAR), jax.random.fold_in(part_keys[3], 1), 0, SHEAR - 1).astype(jnp.int32),
        "scan_x": set_ends(jax.random.randint(part_keys[4], (ANGLE_GROUPS, N_STRIP, M), 0, min(WX, 3 * WX - FRAME - SHEAR + 1)), jax.random.fold_in(part_keys[4], 1), 0, (min(WX, 3 * WX - FRAME - SHEAR + 1)) - 1).astype(jnp.int32),
        "scan_y": set_ends(jax.random.randint(part_keys[5], (ANGLE_GROUPS, N_STRIP, M), 0, NY - FRAME + 1), jax.random.fold_in(part_keys[5], 1), 0, NY - FRAME).astype(jnp.int32),
        "slot_angle": set_ends(jax.random.randint(part_keys[6], (ANGLE_GROUPS, N_STRIP, M), 0, ANG_DEV), jax.random.fold_in(part_keys[6], 1), 0, ANG_DEV - 1).astype(jnp.int32),
        "owner_slot": jax.vmap(lambda own: jax.random.permutation(own, M))(jax.random.split(part_keys[7], ANGLE_GROUPS * N_STRIP)).reshape((ANGLE_GROUPS, N_STRIP, M)).astype(jnp.int32),
        "counts": set_ends(jax.random.randint(part_keys[8], (ANGLE_GROUPS, N_STRIP), M // 2, M + 1), jax.random.fold_in(part_keys[8], 1), M // 2, M).astype(jnp.int32),
    }


def spot(*values):
    return tuple((jnp.asarray(value, jnp.int32) for value in values))

def dft_parts():
    index_row = jnp.arange(FRAME, dtype=jnp.int32)
    wound = index_row[:, None] * index_row[None, :] % FRAME
    phase = wound.astype(jnp.float32) * (2.0 * math.pi / FRAME)
    scaling = 1.0 / math.sqrt(FRAME)
    return ((jnp.cos(phase) * scaling).astype(jnp.bfloat16), (-jnp.sin(phase) * scaling).astype(jnp.bfloat16))

def stamp(value):
    return lax.optimization_barrier(value.astype(jnp.bfloat16)).astype(jnp.float32)

def complex_times(left, right, sign):
    out_re = left[0] * right[0] - sign * left[1] * right[1]
    out_im = left[0] * right[1] + sign * left[1] * right[0]
    return jnp.stack([out_re, out_im], axis=0)

def right_product(block, table_re, table_im, sign):
    part_re = block[0]
    part_im = block[1]
    first = jnp.dot(part_re, table_re, preferred_element_type=jnp.float32)
    second = jnp.dot(part_im, table_im, preferred_element_type=jnp.float32)
    third = jnp.dot(part_re, table_im, preferred_element_type=jnp.float32)
    fourth = jnp.dot(part_im, table_re, preferred_element_type=jnp.float32)
    return jnp.stack([first - sign * second, sign * third + fourth], axis=0)

def row_product(rows_re, rows_im, block, sign):
    part_re = block[0]
    part_im = block[1]
    first = jnp.dot(rows_re, part_re, preferred_element_type=jnp.float32)
    second = jnp.dot(rows_im, part_im, preferred_element_type=jnp.float32)
    third = jnp.dot(rows_im, part_re, preferred_element_type=jnp.float32)
    fourth = jnp.dot(rows_re, part_im, preferred_element_type=jnp.float32)
    return jnp.stack([first - sign * second, sign * third + fourth], axis=0)

def reference(crystal, probe, amplitude, shear, scan_x, scan_y, slot_angle, owner_slot, counts):
    table_re, table_im = dft_parts()
    pad_re = jnp.pad(table_re, ((BAND, BAND), (0, 0)))
    pad_im = jnp.pad(table_im, ((BAND, BAND), (0, 0)))
    probe_pad = jnp.pad(probe, ((0, 0), (BAND, BAND), (0, 0)))
    crystal_pad = jnp.pad(crystal, ((0, 0), (0, 0), (SHEAR, SHEAR), (0, 0)))
    depth_rows = FRAME // N_DEPTH
    quarter = N_STRIP // 4
    band_index = jnp.arange(BAND, dtype=jnp.int32)

    def group_step(summed, group):
        shear_rows = lax.dynamic_slice_in_dim(shear, jnp.asarray(group * ANG_DEV, jnp.int32), ANG_DEV, 0)
        offsets = scan_x[group]
        columns = scan_y[group]
        angles = slot_angle[group]
        owners = owner_slot[group]
        limits = counts[group]

        def pattern_step(gradient_pad, item):
            home = item // M
            slot_id = item % M
            living = (slot_id < limits[home]).astype(jnp.float32)
            offset = offsets[home, slot_id]
            column = columns[home, slot_id]
            quota = owners[home, slot_id]
            owner = (home + 4 * (quota % quarter) + 1) % N_STRIP
            shifts = shear_rows[angles[home, slot_id]]
            starts = [jnp.asarray(band_k * WX - offset - SHEAR + BAND, jnp.int32) for band_k in range(3)]
            rows_re = [lax.dynamic_slice_in_dim(pad_re, first_row, BAND, 0) for first_row in starts]
            rows_im = [lax.dynamic_slice_in_dim(pad_im, first_row, BAND, 0) for first_row in starts]
            probes = [lax.dynamic_slice_in_dim(probe_pad, first_row, BAND, 1).astype(jnp.float32) for first_row in starts]
            spectrum = jnp.zeros((2, FRAME, FRAME), jnp.float32)
            for slab in range(N_DEPTH):
                slab_sum = jnp.zeros((2, FRAME, FRAME), jnp.float32)
                for band_k in range(3):
                    accum = jnp.zeros((2, BAND, FRAME), jnp.float32)
                    for layer_index in range(slab * NZ_DEV, (slab + 1) * NZ_DEV):
                        lift = shifts[layer_index]
                        window = lax.dynamic_slice(crystal_pad[layer_index], spot(0, (home + band_k) * WX + lift, column), (2, BAND, FRAME)).astype(jnp.float32)
                        local_row = band_index + lift - SHEAR
                        inside = ((local_row >= 0) & (local_row < WX)).astype(jnp.float32)
                        accum = accum + window * inside[None, :, None]
                    band = accum.astype(jnp.bfloat16)
                    exit_band = complex_times(probes[band_k], band.astype(jnp.float32), 1.0).astype(jnp.bfloat16)
                    section = right_product(exit_band, table_re, table_im, 1.0).astype(jnp.bfloat16)
                    slab_sum = slab_sum + row_product(rows_re[band_k].T, rows_im[band_k].T, section, 1.0)
                spectrum = spectrum + stamp(slab_sum)
            measured = lax.dynamic_slice(amplitude, spot(group * M + quota, owner * FRAME, 0), (1, FRAME, FRAME))[0].astype(jnp.float32)
            magnitude = jnp.sqrt(spectrum[0] * spectrum[0] + spectrum[1] * spectrum[1])
            factor = (1.0 - measured / jnp.maximum(magnitude, 1.0)) * living
            residual = (spectrum * factor[None]).astype(jnp.bfloat16)
            inverse_rows = right_product(residual, table_re, table_im, -1.0).astype(jnp.bfloat16)
            for band_k in range(3):
                back_total = jnp.zeros((2, BAND, FRAME), jnp.float32)
                for block_index in range(N_DEPTH):
                    row_low = block_index * depth_rows
                    wave = row_product(rows_re[band_k][:, row_low:row_low + depth_rows], rows_im[band_k][:, row_low:row_low + depth_rows], inverse_rows[:, row_low:row_low + depth_rows], -1.0)
                    back_total = back_total + stamp(complex_times(probes[band_k], wave, -1.0))
                back_band = stamp(back_total)
                for layer_index in range(NZ):
                    lift = shifts[layer_index]
                    local_row = band_index + lift - SHEAR
                    inside = ((local_row >= 0) & (local_row < WX)).astype(jnp.float32)
                    position = spot(layer_index, 0, (home + band_k) * WX + lift, column)
                    current = lax.dynamic_slice(gradient_pad, position, (1, 2, BAND, FRAME))
                    gradient_pad = lax.dynamic_update_slice(gradient_pad, current + (back_band * inside[None, :, None])[None], position)
            return (gradient_pad, None)
        items = jnp.arange((N_STRIP - 2) * M, dtype=jnp.int32)
        start_pad = jnp.zeros((NZ, 2, NX + 2 * SHEAR, NY), jnp.float32)
        gradient_pad, unused = lax.scan(pattern_step, start_pad, items)
        cropped = gradient_pad[:, :, SHEAR:SHEAR + NX]
        return (summed + stamp(cropped), None)
    summed, unused = lax.scan(group_step, jnp.zeros((NZ, 2, NX, NY), jnp.float32), jnp.arange(N_ANGLE, dtype=jnp.int32))
    return summed * (1.0 / ANGLES)
```

```python
import functools
import math

import jax
import jax.numpy as jnp
import ml_dtypes
import numpy as np
from jax import lax
from jax.experimental import pallas as pl
from jax.experimental.pallas import tpu as pltpu
from jax.sharding import PartitionSpec as P

BF = jnp.bfloat16
F32 = jnp.float32
VMEM_BYTES = 48 * 2**20
MAX_SHEAR = 16


def dft_table(n):
    index = np.arange(n, dtype=np.int64)
    phase = (index[:, None] * index[None, :] % n).astype(np.float64) * (2.0 * math.pi / n)
    scale = 1.0 / math.sqrt(n)
    table = np.stack([np.cos(phase) * scale, -np.sin(phase) * scale])
    return table.astype(np.float32).astype(ml_dtypes.bfloat16)


def dot(left, right):
    return jnp.dot(left, right, preferred_element_type=F32)


def band_matrix(rows, cols, offset):
    gap = lax.broadcasted_iota(jnp.int32, (rows, cols), 1) - lax.broadcasted_iota(
        jnp.int32, (rows, cols), 0
    )
    return jnp.where(gap == offset, 1.0, 0.0).astype(BF)


def clip(value, top):
    return jnp.minimum(jnp.maximum(value, 0), top)


def slot_of(owner_at, slots, quota):
    found = jnp.int32(0)
    for slot in range(slots):
        found = jnp.where(owner_at(slot) == quota, slot, found)
    return found


def project_kernel(strips, slots, mine, *refs):
    shear, scan_x, scan_y, slot_angle, owner, crystal = refs[:6]
    layers, _, wx, ny = crystal.shape
    if mine:
        arrived, moving, middle, table = refs[6:]
    else:
        (out,) = refs[6:]
    strip = lax.axis_index("strip")
    depth = lax.axis_index("depth")
    half = depth if mine else 1 - depth
    if mine:
        place = 0
        for i in range(shear.shape[0]):
            for z in range(layers):
                table[place] = shear[i, z]
                place += 1
        for ref in (scan_y, slot_angle, owner):
            for i in range(strips):
                for m in range(slots):
                    table[place] = ref[0, i, m]
                    place += 1
    bricks = [
        jnp.concatenate([crystal[z, part] for z in range(layers)], axis=0) for part in range(2)
    ]
    frame = out.shape[-1] if not mine else moving.shape[-1]
    for kind in range(2):
        home = clip(strip - (2 * half if kind == 0 else 1), strips - 1)
        back = wx * half if kind == 0 else wx * (1 - half)
        for quota in range(slots):
            slot = slot_of(lambda m: owner[0, home, m], slots, quota)
            start = scan_x[0, home, slot] - back
            angle = slot_angle[0, home, slot]
            rows = jnp.concatenate(
                [band_matrix(wx, wx, start + shear[angle, z]) for z in range(layers)], axis=1
            )
            columns = band_matrix(ny, frame, -scan_y[0, home, slot])
            for part in range(2):
                lifted = dot(rows, bricks[part]).astype(BF)
                band = dot(lifted, columns)
                if mine:
                    band = band + arrived[kind, quota, part].astype(F32)
                    (moving if kind == 0 else middle)[quota, part] = band.astype(BF)
                else:
                    out[kind, quota, part] = band.astype(BF)


def transform_kernel(strips, angles, slots, window, *refs):
    scan_x, owner, counts = refs[:3]
    moved, moved_far, middle, middle_far, near, far, probe, tab = refs[3:11]
    outs = refs[11 : 11 + 2 * angles]
    waves, levels = refs[11 + 2 * angles :]
    quarter = strips // 4
    strip = lax.axis_index("strip")
    plane = lax.axis_index("angle")
    depth = lax.axis_index("depth")
    half = moved.shape[2]
    frame = moved.shape[3]
    f_re = tab[0]
    f_im = tab[1]
    n_im = -f_im
    for quota in range(slots):
        home = lax.rem(strip + (strips - 1) + 4 * (strips - quota % quarter), strips)
        slot = slot_of(lambda m: owner[0, home, m], slots, quota)
        alive = jnp.logical_and(home <= strips - 3, slot < counts[0, home])
        alive = jnp.where(alive, 1.0, 0.0).astype(F32)
        for side, (a_ref, m_ref) in enumerate(((moved, middle), (moved_far, middle_far))):
            row = pl.multiple_of((depth if side == 0 else 1 - depth) * half, half)
            w_re = a_ref[quota, 0].astype(F32) + m_ref[quota, 0].astype(F32)
            w_im = a_ref[quota, 1].astype(F32) + m_ref[quota, 1].astype(F32)
            p_re = probe[0, pl.ds(row, half)].astype(F32)
            p_im = probe[1, pl.ds(row, half)].astype(F32)
            waves[quota, pl.ds(row, half), :frame] = (p_re * w_re - p_im * w_im).astype(BF)
            waves[quota, pl.ds(row, half), frame:] = (p_re * w_im + p_im * w_re).astype(BF)
        exit_wave = waves[quota]
        section = jnp.concatenate(
            [
                dot(exit_wave, jnp.concatenate([f_re, n_im], axis=0)).astype(BF),
                dot(exit_wave, jnp.concatenate([f_im, f_re], axis=0)).astype(BF),
            ],
            axis=0,
        )
        s_re = dot(jnp.concatenate([f_re, n_im], axis=1), section)
        s_im = dot(jnp.concatenate([f_im, f_re], axis=1), section)
        magnitude = jnp.maximum(jnp.sqrt(s_re * s_re + s_im * s_im), 1.0)
        for side, a_ref in enumerate((near, far)):
            row = pl.multiple_of((depth if side == 0 else 1 - depth) * half, half)
            levels[quota, pl.ds(row, half)] = a_ref[quota]
        measured = levels[quota].astype(F32)
        factor = (1.0 - measured / magnitude) * alive
        residual = jnp.concatenate(
            [(s_re * factor).astype(BF), (s_im * factor).astype(BF)], axis=1
        )
        inverse = jnp.concatenate(
            [
                dot(residual, jnp.concatenate([f_re, f_im], axis=0)).astype(BF),
                dot(residual, jnp.concatenate([n_im, f_re], axis=0)).astype(BF),
            ],
            axis=0,
        )
        b_re = dot(jnp.concatenate([f_re, f_im], axis=1), inverse)
        b_im = dot(jnp.concatenate([n_im, f_re], axis=1), inverse)
        p_re = probe[0].astype(F32)
        p_im = probe[1].astype(F32)
        back = jnp.concatenate(
            [
                (p_re * b_re + p_im * b_im).astype(BF),
                (p_re * b_im - p_im * b_re).astype(BF),
            ],
            axis=1,
        )
        offset = scan_x[0, home, slot]
        share = window - MAX_SHEAR
        for shift in range(angles):
            target = lax.rem(plane + shift, angles)
            for kind in range(2):
                reach = 2 * depth if kind == 0 else 1
                first = reach * (share * angles) + share * target - offset - MAX_SHEAR
                cut = dot(band_matrix(window, frame, first), back).astype(BF)
                outs[2 * shift + kind][quota, 0] = cut[:, :frame]
                outs[2 * shift + kind][quota, 1] = cut[:, frame:]


def deposit_kernel(strips, angles, slots, scale, *refs):
    tables = refs[:angles]
    blocks = refs[angles : angles + 3 * angles]
    (out,) = refs[4 * angles :]
    layers, _, share, ny = out.shape
    window, frame = blocks[0].shape[2:]
    strip = lax.axis_index("strip")
    depth = lax.axis_index("depth")
    count = strips * slots
    rows = []
    values = ([], [])
    for shift in range(angles):
        table = tables[shift]
        base = table.shape[0] - 3 * count
        for kind in range(3):
            reach = (2 * depth, 2 - 2 * depth, 1)[kind]
            home = clip(strip - reach, strips - 1)
            block = blocks[3 * shift + kind]
            for quota in range(slots):
                slot = slot_of(
                    lambda m: table[base + 2 * count + home * slots + m], slots, quota
                )
                column = table[base + home * slots + slot]
                angle = table[base + count + home * slots + slot]
                rows.append(
                    jnp.concatenate(
                        [
                            band_matrix(share, window, MAX_SHEAR - table[angle * layers + z])
                            for z in range(layers)
                        ],
                        axis=0,
                    )
                )
                columns = band_matrix(frame, ny, column)
                for part in range(2):
                    values[part].append(dot(block[quota, part], columns).astype(BF))
    left = jnp.concatenate(rows, axis=1)
    for part in range(2):
        total = dot(left, jnp.concatenate(values[part], axis=0)) * scale
        for z in range(layers):
            out[z, part] = total[z * share : (z + 1) * share]


def body(mesh_shape, crystal, probe, amplitude, shear, scan_x, scan_y, slot_angle, owner_slot, counts):
    strips, angles, depths = (mesh_shape[n] for n in ("strip", "angle", "depth"))
    slots = owner_slot.shape[2]
    quarter = strips // 4
    lanes = slots // quarter
    layers, _, wx, ny = crystal.shape
    frame = probe.shape[-1]
    share = wx // angles
    window = share + MAX_SHEAR
    half = amplitude.shape[1]
    axes = ("strip", "angle", "depth")
    params = pltpu.CompilerParams(vmem_limit_bytes=VMEM_BYTES)
    smem = pl.BlockSpec(memory_space=pltpu.SMEM)
    vmem = pl.BlockSpec(memory_space=pltpu.VMEM)

    def swap(x):
        return lax.ppermute(x, "depth", [(d, (d + 1) % depths) for d in range(depths)])

    def permute(x, move):
        pairs = []
        for s in range(strips):
            for a in range(angles):
                for d in range(depths):
                    to = move(s, a, d)
                    if to is not None:
                        pairs.append(
                            (
                                (s * angles + a) * depths + d,
                                (to[0] * angles + to[1]) * depths + to[2],
                            )
                        )
        return lax.ppermute(x, axes, pairs)

    def ring(x, turn, lap):
        def move(s, a, d):
            a = (a + lap) % angles
            way = turn if d == 0 else -turn
            if 0 <= s + way < strips:
                return s + way, a, d
            return s, a, 1 - d

        return permute(x, move)

    def far(x, way, lap, hops, forward):
        def move(s, a, d):
            reach = 2 * d if way else 1
            home = s - reach if forward else (s - 1 - 4 * hops) % strips
            if not 0 <= home <= strips - 3:
                return None
            to = (home + 1 + 4 * hops) % strips if forward else home + reach
            return to, (a + lap) % angles, d

        return permute(x, move)

    amplitude_far = swap(amplitude)
    ints = (shear, scan_x, scan_y, slot_angle, owner_slot)
    halves = jax.ShapeDtypeStruct((slots, 2, half, frame), BF)
    sent = pl.pallas_call(
        functools.partial(project_kernel, strips, slots, False),
        out_shape=jax.ShapeDtypeStruct((2, slots, 2, half, frame), BF),
        in_specs=[smem] * 5 + [vmem],
        out_specs=vmem,
        compiler_params=params,
        name="project_far",
    )(*ints, crystal)
    arrived = swap(sent)
    entries = shear.shape[0] * layers + 3 * strips * slots
    moving, middle, table = pl.pallas_call(
        functools.partial(project_kernel, strips, slots, True),
        out_shape=[halves, halves, jax.ShapeDtypeStruct((entries,), jnp.int32)],
        in_specs=[smem] * 5 + [vmem] * 2,
        out_specs=[vmem, vmem, smem],
        compiler_params=params,
        name="project_near",
    )(*ints, crystal, arrived)
    tables = [table] + [
        lax.ppermute(table, "angle", [(a, (a + t) % angles) for a in range(angles)])
        for t in range(1, angles)
    ]

    def by_hops(x, near, beyond):
        if quarter == 1:
            return near(x)
        pieces = []
        for hops in range(quarter):
            piece = x[hops::quarter]
            pieces.append(near(piece) if hops == 0 else beyond(piece, hops))
        return jnp.stack(pieces, axis=1).reshape(x.shape)

    moved = by_hops(moving, lambda x: ring(x, 1, 0), lambda x, n: far(x, 1, 0, n, True))
    middle = by_hops(middle, lambda x: x, lambda x, n: far(x, 0, 0, n, True))
    middle_far = swap(middle)
    moved_far = swap(moved)
    cuts = pl.pallas_call(
        functools.partial(transform_kernel, strips, angles, slots, window),
        out_shape=[jax.ShapeDtypeStruct((slots, 2, window, frame), BF)] * (2 * angles),
        in_specs=[smem] * 3 + [vmem] * 8,
        out_specs=[vmem] * (2 * angles),
        scratch_shapes=[
            pltpu.VMEM((slots, frame, 2 * frame), BF),
            pltpu.VMEM((slots, frame, frame), BF),
        ],
        compiler_params=params,
        name="transform",
    )(
        scan_x, owner_slot, counts, moved, moved_far, middle, middle_far,
        amplitude, amplitude_far, probe, jnp.asarray(dft_table(frame)),
    )
    blocks = []
    for lap in range(angles):
        outer = by_hops(
            cuts[2 * lap],
            lambda x: ring(x, -1, lap),
            lambda x, n: far(x, 1, lap, n, False),
        )
        inner = by_hops(
            cuts[2 * lap + 1],
            lambda x: x
            if lap == 0
            else lax.ppermute(x, "angle", [(a, (a + lap) % angles) for a in range(angles)]),
            lambda x, n: far(x, 0, lap, n, False),
        )
        blocks += [outer, swap(outer), inner]
    scale = 1.0 / (shear.shape[0] * angles)
    return pl.pallas_call(
        functools.partial(deposit_kernel, strips, angles, slots, scale),
        out_shape=jax.ShapeDtypeStruct((layers, 2, share, ny), F32),
        in_specs=[smem] * angles + [vmem] * (3 * angles),
        out_specs=vmem,
        compiler_params=params,
        name="deposit",
    )(*tables, *blocks)


def solution(mesh):
    placed = (
        P(("groups", "depth"), None, "strip", None),
        P(),
        P("angle", ("groups", "strip", "depth"), None),
        P(("groups", "angle"), "depth"),
        P(("groups", "angle"), None, None),
        P(("groups", "angle"), None, None),
        P(("groups", "angle"), None, None),
        P(("groups", "angle"), None, None),
        P(("groups", "angle"), None),
    )
    return jax.shard_map(
        functools.partial(body, dict(mesh.shape)),
        mesh=mesh,
        in_specs=placed,
        out_specs=P(("groups", "depth"), None, ("strip", "angle"), None),
        check_vma=False,
    )
```

```python
import functools
import math

import jax
import jax.numpy as jnp
import ml_dtypes
import numpy as np
from jax import lax
from jax.experimental import pallas as pl
from jax.experimental.pallas import tpu as pltpu
from jax.sharding import PartitionSpec as P

BF = jnp.bfloat16
F32 = jnp.float32
VMEM_BYTES = 48 * 2**20
MAX_SHEAR = 16


def dft_table(n):
    index = np.arange(n, dtype=np.int64)
    phase = (index[:, None] * index[None, :] % n).astype(np.float64) * (2.0 * math.pi / n)
    scale = 1.0 / math.sqrt(n)
    table = np.stack([np.cos(phase) * scale, -np.sin(phase) * scale])
    return table.astype(np.float32).astype(ml_dtypes.bfloat16)


def dot(left, right):
    return jnp.dot(left, right, preferred_element_type=F32)


def band_matrix(rows, cols, offset):
    gap = lax.broadcasted_iota(jnp.int32, (rows, cols), 1) - lax.broadcasted_iota(
        jnp.int32, (rows, cols), 0
    )
    return jnp.where(gap == offset, 1.0, 0.0).astype(BF)


def clip(value, top):
    return jnp.minimum(jnp.maximum(value, 0), top)


class Table:
    def __init__(self, ref, strips, slots, layers):
        self.ref, self.slots, self.layers = ref, slots, layers
        self.count = strips * slots
        self.base = ref.shape[0] - 4 * self.count - strips

    def pick(self, which, home, slot):
        return self.ref[self.base + which * self.count + home * self.slots + slot]

    def column(self, home, slot):
        return self.pick(0, home, slot)

    def shears(self, home, slot):
        angle = self.pick(1, home, slot)
        return [self.ref[angle * self.layers + z] for z in range(self.layers)]

    def slot(self, home, quota):
        found = jnp.int32(0)
        for slot in range(self.slots):
            found = jnp.where(self.pick(2, home, slot) == quota, slot, found)
        return found

    def offset(self, home, slot):
        return self.pick(3, home, slot)

    def alive(self, home, slot):
        return slot < self.ref[self.base + 4 * self.count + home]


def fill_table(table, shear, by_slot, counts):
    place = 0
    for i in range(shear.shape[0]):
        for z in range(shear.shape[1]):
            table[place] = shear[i, z]
            place += 1
    _, slots, strips = by_slot[0].shape
    for ref in by_slot:
        for home in range(strips):
            for slot in range(slots):
                table[place] = ref[0, slot, home]
                place += 1
    for home in range(strips):
        table[place] = counts[0, home]
        place += 1


def project_kernel(strips, slots, mine, *refs):
    strip = lax.axis_index("strip")
    depth = lax.axis_index("depth")
    half = depth if mine else 1 - depth
    if mine:
        table, crystal, *parts = refs
    else:
        shear, scan_x, scan_y, slot_angle, owner, counts, crystal, *parts, table = refs
        fill_table(table, shear, (scan_y, slot_angle, owner, scan_x), counts)
    layers, _, wx, ny = crystal.shape
    ints = Table(table, strips, slots, layers)
    frame = parts[0].shape[-1]
    rows = []
    columns = []
    for kind, out in enumerate(parts):
        home = clip(strip - (2 * half if kind == 0 else 1), strips - 1)
        back = wx * half if kind == 0 else wx
        for quota in range(slots):
            slot = ints.slot(home, quota)
            start = ints.offset(home, slot) - back
            rows.append(
                jnp.concatenate(
                    [
                        band_matrix(out.shape[2], wx, start + shear)
                        for shear in ints.shears(home, slot)
                    ],
                    axis=1,
                )
            )
            columns.append(band_matrix(ny, frame, -ints.column(home, slot)))
    rows = jnp.concatenate(rows, axis=0)
    lifted = [
        dot(rows, jnp.concatenate([crystal[z, part] for z in range(layers)], axis=0)).astype(BF)
        for part in range(2)
    ]
    place = 0
    for kind, out in enumerate(parts):
        tall = out.shape[2]
        for quota in range(slots):
            both = jnp.concatenate([x[place : place + tall] for x in lifted], axis=0)
            band = dot(both, columns[kind * slots + quota]).astype(out.dtype)
            out[quota, 0] = band[:tall]
            out[quota, 1] = band[tall:]
            place += tall


def add_kernel(near, far, out):
    out[...] = (near[...] + far[...].astype(F32)).astype(out.dtype)


def transform_kernel(strips, angles, slots, layers, window, *refs):
    table, moved, moved_far, middle, middle_far, near, far, probe, tab = refs[:9]
    ints = Table(table, strips, slots, layers)
    outs = refs[9 : 9 + 2 * angles]
    waves, levels = refs[9 + 2 * angles :]
    quarter = strips // 4
    strip = lax.axis_index("strip")
    plane = lax.axis_index("angle")
    depth = lax.axis_index("depth")
    half = moved.shape[2]
    frame = moved.shape[3]
    f_re = tab[0]
    f_im = tab[1]
    n_im = -f_im
    homes = []
    places = []
    for quota in range(slots):
        home = lax.rem(strip + (strips - 1) + 4 * (strips - quota % quarter), strips)
        homes.append(home)
        places.append(ints.slot(home, quota))
        for side, (a_ref, level) in enumerate(((moved, near), (moved_far, far))):
            row = pl.multiple_of((depth if side == 0 else 1 - depth) * half, half)
            here = pl.ds(row, half)
            w_re, w_im = (
                a_ref[quota, part].astype(F32)
                + middle[quota, part, here].astype(F32)
                + middle_far[quota, part, here].astype(F32)
                for part in range(2)
            )
            p_re = probe[0, here].astype(F32)
            p_im = probe[1, here].astype(F32)
            to = pl.ds(row + quota * frame, half)
            waves[to, :frame] = (p_re * w_re - p_im * w_im).astype(BF)
            waves[to, frame:] = (p_re * w_im + p_im * w_re).astype(BF)
            levels[quota, here] = level[quota]

    def side_by_side(x, dtype=BF):
        return jnp.concatenate(
            [
                jnp.concatenate(
                    [
                        x[q * frame : (q + 1) * frame, p * frame : (p + 1) * frame]
                        for q in range(slots)
                    ],
                    axis=1,
                )
                for p in range(2)
            ],
            axis=0,
        ).astype(dtype)

    def blocks(re, im, low):
        return jnp.concatenate(
            [jnp.concatenate([re, im], axis=1), jnp.concatenate([low, re], axis=1)], axis=0
        )

    ahead = blocks(f_re, f_im, n_im)
    behind = blocks(f_re, n_im, f_im)
    section = side_by_side(dot(waves[...], ahead))
    spectrum = dot(behind, section)
    p_re = probe[0].astype(F32)
    p_im = probe[1].astype(F32)
    residuals = []
    for quota in range(slots):
        alive = jnp.logical_and(
            homes[quota] <= strips - 3, ints.alive(homes[quota], places[quota])
        )
        alive = jnp.where(alive, 1.0, 0.0).astype(F32)
        s_re = spectrum[:frame, quota * frame : (quota + 1) * frame]
        s_im = spectrum[frame:, quota * frame : (quota + 1) * frame]
        magnitude = jnp.maximum(jnp.sqrt(s_re * s_re + s_im * s_im), 1.0)
        factor = (1.0 - levels[quota].astype(F32) / magnitude) * alive
        residuals.append(jnp.concatenate([s_re * factor, s_im * factor], axis=1).astype(BF))
    inverse = side_by_side(dot(jnp.concatenate(residuals, axis=0), behind))
    wave = dot(ahead, inverse)
    share = window - MAX_SHEAR
    for quota in range(slots):
        b_re = wave[:frame, quota * frame : (quota + 1) * frame]
        b_im = wave[frame:, quota * frame : (quota + 1) * frame]
        back = jnp.concatenate(
            [p_re * b_re + p_im * b_im, p_re * b_im - p_im * b_re], axis=1
        ).astype(BF)
        offset = ints.offset(homes[quota], places[quota])
        picks = []
        for shift in range(angles):
            target = lax.rem(plane + shift, angles)
            for kind in range(2):
                reach = 2 * depth if kind == 0 else 1
                first = reach * (share * angles) + share * target - offset - MAX_SHEAR
                picks.append(band_matrix(window, frame, first))
        cut = dot(jnp.concatenate(picks, axis=0), back).astype(BF)
        for place, out in enumerate(outs):
            rows = cut[place * window : (place + 1) * window]
            held = out.shape[0]
            if held == slots:
                out[quota, 0] = rows[:, :frame]
                out[quota, 1] = rows[:, frame:]
                continue

            @pl.when(depth == quota // held)
            def _():
                out[quota % held, 0] = rows[:, :frame]
                out[quota % held, 1] = rows[:, frame:]


def deposit_kernel(strips, slots, items, before, last, scale, *refs):
    laps = sorted({lap for lap, _ in items})
    tables = dict(zip(laps, refs))
    refs = refs[len(laps) :]
    blocks, refs = refs[: len(items)], refs[len(items) :]
    sums = refs[0] if before else None
    out = refs[1] if before else refs[0]
    total, sems = refs[-2:] if last else (out, None)
    layers, _, share, ny = out.shape
    window, frame = blocks[0].shape[2:]
    strip = lax.axis_index("strip")
    depth = lax.axis_index("depth")
    rows = []
    values = ([], [])
    for (lap, kind), block in zip(items, blocks):
        ints = Table(tables[lap], strips, slots, layers)
        reach = (2 * depth, 2 - 2 * depth, 1, 1)[kind]
        home = clip(strip - reach, strips - 1)
        held = block.shape[0]
        for place in range(held):
            quota = place
            if held < slots:
                quota = place + held * (depth if kind == 2 else 1 - depth)
            slot = ints.slot(home, quota)
            rows.append(
                jnp.concatenate(
                    [
                        band_matrix(share, window, MAX_SHEAR - shear)
                        for shear in ints.shears(home, slot)
                    ],
                    axis=0,
                )
            )
            columns = band_matrix(frame, ny, ints.column(home, slot))
            both = jnp.concatenate([block[place, 0], block[place, 1]], axis=0)
            placed = dot(both, columns).astype(BF)
            values[0].append(placed[:window])
            values[1].append(placed[window:])
    left = jnp.concatenate(rows, axis=1)
    copies = []
    for part in range(2):
        grown = dot(left, jnp.concatenate(values[part], axis=0)) * scale
        for z in range(layers):
            piece = grown[z * share : (z + 1) * share]
            total[z, part] = piece if sums is None else piece + sums[z, part]
            if last:
                copies.append(
                    pltpu.make_async_copy(total.at[z, part], out.at[z, part], sems.at[z, part])
                )
                copies[-1].start()
    for copy in copies:
        copy.wait()


def body(mesh_shape, crystal, probe, amplitude, shear, scan_x, scan_y, slot_angle, owner_slot, counts):
    strips, angles, depths = (mesh_shape[n] for n in ("strip", "angle", "depth"))
    slots = owner_slot.shape[2]
    quarter = strips // 4
    lanes = slots // quarter
    layers, _, wx, ny = crystal.shape
    frame = probe.shape[-1]
    share = wx // angles
    window = share + MAX_SHEAR
    half = amplitude.shape[1]
    axes = ("strip", "angle", "depth")
    params = pltpu.CompilerParams(vmem_limit_bytes=VMEM_BYTES)
    smem = pl.BlockSpec(memory_space=pltpu.SMEM)
    vmem = pl.BlockSpec(memory_space=pltpu.VMEM)

    def cost(micros):
        return pl.CostEstimate(flops=int(micros * 8e8), bytes_accessed=0, transcendentals=0)

    def swap(x):
        return lax.ppermute(x, "depth", [(d, (d + 1) % depths) for d in range(depths)])

    def permute(x, move):
        pairs = []
        for s in range(strips):
            for a in range(angles):
                for d in range(depths):
                    to = move(s, a, d)
                    if to is not None:
                        pairs.append(
                            (
                                (s * angles + a) * depths + d,
                                (to[0] * angles + to[1]) * depths + to[2],
                            )
                        )
        return lax.ppermute(x, axes, pairs)

    def ring(x, turn, lap):
        def move(s, a, d):
            way = turn if d == 0 else -turn
            if 0 <= s + way < strips:
                return s + way, (a + lap) % angles, d
            return s, a, 1 - d

        return permute(x, move)

    def far(x, way, lap, hops, forward):
        def move(s, a, d):
            reach = 2 * d if way else 1
            home = s - reach if forward else (s - 1 - 4 * hops) % strips
            if not 0 <= home <= strips - 3:
                return None
            to = (home + 1 + 4 * hops) % strips if forward else home + reach
            return to, (a + lap) % angles, d

        return permute(x, move)

    amplitude_far = swap(amplitude)
    flat = [jnp.swapaxes(x, 1, 2) for x in (scan_x, scan_y, slot_angle, owner_slot)]
    ints = (shear, *flat, counts)
    entries = shear.shape[0] * layers + 4 * strips * slots + strips
    sent, table = pl.pallas_call(
        functools.partial(project_kernel, strips, slots, False),
        out_shape=[
            jax.ShapeDtypeStruct((slots, 2, half, frame), BF),
            jax.ShapeDtypeStruct((entries,), jnp.int32),
        ],
        in_specs=[smem] * 6 + [vmem],
        out_specs=[vmem, smem],
        compiler_params=params,
        cost_estimate=cost(1.5),
        name="project_far",
    )(*ints, crystal)
    arrived = swap(sent)
    tables = [table] + [
        lax.ppermute(table, "angle", [(a, (a + t) % angles) for a in range(angles)])
        for t in range(1, angles)
    ]
    moving, middle = pl.pallas_call(
        functools.partial(project_kernel, strips, slots, True),
        out_shape=[
            jax.ShapeDtypeStruct((slots, 2, half, frame), F32),
            jax.ShapeDtypeStruct((slots, 2, frame, frame), BF),
        ],
        in_specs=[smem, vmem],
        out_specs=[vmem, vmem],
        compiler_params=params,
        cost_estimate=cost(2.5),
        name="project_near",
    )(table, crystal)
    moving = pl.pallas_call(
        add_kernel,
        out_shape=jax.ShapeDtypeStruct(moving.shape, BF),
        in_specs=[vmem] * 2,
        out_specs=vmem,
        compiler_params=params,
        cost_estimate=cost(0.5),
        name="add",
    )(moving, arrived)

    def by_hops(x, near, beyond):
        if quarter == 1:
            return near(x)
        pieces = []
        for hops in range(quarter):
            piece = x[hops::quarter]
            pieces.append(near(piece) if hops == 0 else beyond(piece, hops))
        return jnp.stack(pieces, axis=1).reshape(x.shape)

    moved = by_hops(moving, lambda x: ring(x, 1, 0), lambda x, n: far(x, 1, 0, n, True))
    middle = by_hops(middle, lambda x: x, lambda x, n: far(x, 0, 0, n, True))
    middle_far = swap(middle)
    moved, tables, amplitude_far = lax.optimization_barrier((moved, tables, amplitude_far))
    moved_far = swap(moved)
    split = quarter == 1 and slots % depths == 0
    held = slots // depths if split else slots
    cuts = pl.pallas_call(
        functools.partial(transform_kernel, strips, angles, slots, layers, window),
        out_shape=[
            jax.ShapeDtypeStruct((held if i > 1 and i % 2 else slots, 2, window, frame), BF)
            for i in range(2 * angles)
        ],
        in_specs=[smem] + [vmem] * 8,
        out_specs=[vmem] * (2 * angles),
        scratch_shapes=[
            pltpu.VMEM((slots * frame, 2 * frame), BF),
            pltpu.VMEM((slots, frame, frame), BF),
        ],
        compiler_params=params,
        cost_estimate=cost(3),
        name="transform",
    )(
        table, moved, moved_far, middle, middle_far,
        amplitude, amplitude_far, probe, jnp.asarray(dft_table(frame)),
    )
    blocks = {}
    for lap in range(angles):
        blocks[lap, 0] = by_hops(
            cuts[2 * lap],
            lambda x: ring(x, -1, lap),
            lambda x, n: far(x, 1, lap, n, False),
        )
        blocks[lap, 2] = by_hops(
            cuts[2 * lap + 1],
            lambda x: x
            if lap == 0
            else lax.ppermute(x, "angle", [(a, (a + lap) % angles) for a in range(angles)]),
            lambda x, n: far(x, 0, lap, n, False),
        )
    scale = 1.0 / (shear.shape[0] * angles)

    def deposit(items, sums, last):
        laps = sorted({lap for lap, _ in items})
        sums = [] if sums is None else [sums]
        shape = (layers, 2, share, ny)
        return pl.pallas_call(
            functools.partial(deposit_kernel, strips, slots, items, bool(sums), last, scale),
            out_shape=jax.ShapeDtypeStruct(shape, F32),
            in_specs=[smem] * len(laps) + [vmem] * (len(items) + len(sums)),
            out_specs=pl.BlockSpec(memory_space=pltpu.HBM) if last else vmem,
            scratch_shapes=[pltpu.VMEM(shape, F32), pltpu.SemaphoreType.DMA((layers, 2))]
            if last
            else [],
            compiler_params=params,
            cost_estimate=cost(0.05),
            name="deposit",
        )(*(tables[lap] for lap in laps), *(blocks[item] for item in items), *sums)

    later = range(1, angles)
    keys = [(lap, 0) for lap in range(angles)] + [(lap, 2) for lap in later]
    blocks.update(zip(keys, lax.optimization_barrier([blocks[key] for key in keys])))
    shared = {0: 1, 2: 3} if split else {0: 1}
    others = [(lap, shared[kind]) for lap, kind in keys if kind in shared]
    blocks.update({(lap, shared[kind]): swap(blocks[lap, kind]) for lap, kind in keys if kind in shared})
    return deposit(others, deposit(keys + [(0, 2)], None, False), True)


def solution(mesh):
    placed = (
        P(("groups", "depth"), None, "strip", None),
        P(),
        P("angle", ("groups", "strip", "depth"), None),
        P(("groups", "angle"), "depth"),
        P(("groups", "angle"), None, None),
        P(("groups", "angle"), None, None),
        P(("groups", "angle"), None, None),
        P(("groups", "angle"), None, None),
        P(("groups", "angle"), None),
    )
    return jax.shard_map(
        functools.partial(body, dict(mesh.shape)),
        mesh=mesh,
        in_specs=placed,
        out_specs=P(("groups", "depth"), None, ("strip", "angle"), None),
        check_vma=False,
    )
```

```python
import functools
import math

import jax
import jax.numpy as jnp
import ml_dtypes
import numpy as np
from jax import lax
from jax.experimental import pallas as pl
from jax.experimental.pallas import tpu as pltpu
from jax.sharding import PartitionSpec as P

BF = jnp.bfloat16
F32 = jnp.float32
VMEM_BYTES = 48 * 2**20
FILL_VMEM_BYTES = 54 * 2**20
MAX_SHEAR = 16


def dft_tables(n):
    index = np.arange(n, dtype=np.int64)
    phase = (index[:, None] * index[None, :] % n).astype(np.float64) * (2.0 * math.pi / n)
    scale = 1.0 / math.sqrt(n)
    re, im = np.cos(phase) * scale, -np.sin(phase) * scale
    tables = np.stack([np.block([[re, im], [-im, re]]), np.block([[re, -im], [im, re]])])
    return tables.astype(np.float32).astype(ml_dtypes.bfloat16)


def dot(left, right):
    return jnp.dot(left, right, preferred_element_type=F32)


def band_matrix(rows, cols, offset):
    gap = lax.broadcasted_iota(jnp.int32, (rows, cols), 1) - lax.broadcasted_iota(
        jnp.int32, (rows, cols), 0
    )
    return jnp.where(gap == offset, 1.0, 0.0).astype(BF)


def clip(value, top):
    return jnp.minimum(jnp.maximum(value, 0), top)


class Table:
    def __init__(self, ref, strips, slots, layers):
        self.ref, self.slots, self.layers = ref, slots, layers
        self.count = strips * slots
        self.base = ref.shape[0] - 4 * self.count - strips

    def pick(self, which, home, slot):
        return self.ref[self.base + which * self.count + home * self.slots + slot]

    def column(self, home, slot):
        return self.pick(0, home, slot)

    def shears(self, home, slot):
        angle = self.pick(1, home, slot)
        return [self.ref[angle * self.layers + z] for z in range(self.layers)]

    def slot(self, home, quota):
        found = jnp.int32(0)
        for slot in range(self.slots):
            found = jnp.where(self.pick(2, home, slot) == quota, slot, found)
        return found

    def offset(self, home, slot):
        return self.pick(3, home, slot)

    def alive(self, home, slot):
        return slot < self.ref[self.base + 4 * self.count + home]


def fill_kernel(shear, scan_x, scan_y, slot_angle, owner, counts, table):
    place = 0
    for i in range(shear.shape[0]):
        for z in range(shear.shape[1]):
            table[place] = shear[i, z]
            place += 1
    _, slots, strips = scan_x.shape
    for ref in (scan_y, slot_angle, owner, scan_x):
        for home in range(strips):
            for slot in range(slots):
                table[place] = ref[0, slot, home]
                place += 1
    for home in range(strips):
        table[place] = counts[0, home]
        place += 1


def project_kernel(strips, slots, mine, *refs):
    strip = lax.axis_index("strip")
    depth = lax.axis_index("depth")
    half = depth if mine else 1 - depth
    table, crystal, *parts = refs
    layers, _, wx, ny = crystal.shape
    ints = Table(table, strips, slots, layers)
    frame = parts[0].shape[-1]
    rows = []
    columns = []
    for kind, out in enumerate(parts):
        home = clip(strip - (2 * half if kind == 0 else 1), strips - 1)
        back = wx * half if kind == 0 else wx
        for quota in range(slots):
            slot = ints.slot(home, quota)
            start = ints.offset(home, slot) - back
            rows.append(
                jnp.concatenate(
                    [
                        band_matrix(out.shape[2], wx, start + shear)
                        for shear in ints.shears(home, slot)
                    ],
                    axis=1,
                )
            )
            columns.append(band_matrix(ny, frame, -ints.column(home, slot)))
    rows = jnp.concatenate(rows, axis=0)
    lifted = [
        dot(rows, jnp.concatenate([crystal[z, part] for z in range(layers)], axis=0)).astype(BF)
        for part in range(2)
    ]
    place = 0
    for kind, out in enumerate(parts):
        tall = out.shape[2]
        for quota in range(slots):
            both = jnp.concatenate([x[place : place + tall] for x in lifted], axis=0)
            band = dot(both, columns[kind * slots + quota]).astype(out.dtype)
            out[quota, 0] = band[:tall]
            out[quota, 1] = band[tall:]
            place += tall


def add_kernel(near, far, out):
    out[...] = (near[...] + far[...].astype(F32)).astype(out.dtype)


def cut_kernel(strips, angles, slots, layers, window, table, picks, alive):
    ints = Table(table, strips, slots, layers)
    quarter = strips // 4
    strip = lax.axis_index("strip")
    plane = lax.axis_index("angle")
    depth = lax.axis_index("depth")
    share = window - MAX_SHEAR
    for quota in range(slots):
        home = lax.rem(strip + (strips - 1) + 4 * (strips - quota % quarter), strips)
        slot = ints.slot(home, quota)
        live = jnp.logical_and(home <= strips - 3, ints.alive(home, slot))
        alive[quota] = jnp.full(alive.shape[1:], jnp.where(live, 1.0, 0.0), F32)
        offset = ints.offset(home, slot)
        for shift in range(angles):
            target = lax.rem(plane + shift, angles)
            for kind in range(2):
                reach = 2 * depth if kind == 0 else 1
                first = reach * (share * angles) + share * target - offset - MAX_SHEAR
                place = (2 * shift + kind) * window
                picks[quota, place : place + window] = band_matrix(window, picks.shape[2], first)


def transform_kernel(angles, slots, window, *refs):
    moved, moved_far, middle, middle_far, near, far, probe, tab, picks, alive = refs[:10]
    outs = refs[10 : 10 + 2 * angles]
    waves, levels = refs[10 + 2 * angles :]
    depth = lax.axis_index("depth")
    half = moved.shape[2]
    frame = moved.shape[3]
    for quota in range(slots):
        for side, (a_ref, level) in enumerate(((moved, near), (moved_far, far))):
            row = pl.multiple_of((depth if side == 0 else 1 - depth) * half, half)
            here = pl.ds(row, half)
            w_re, w_im = (
                a_ref[quota, part].astype(F32)
                + middle[quota, part, here].astype(F32)
                + middle_far[quota, part, here].astype(F32)
                for part in range(2)
            )
            p_re = probe[0, here].astype(F32)
            p_im = probe[1, here].astype(F32)
            to = pl.ds(row + quota * frame, half)
            waves[to, :frame] = (p_re * w_re - p_im * w_im).astype(BF)
            waves[to, frame:] = (p_re * w_im + p_im * w_re).astype(BF)
            levels[quota, here] = level[quota]

    def side_by_side(x, dtype=BF):
        return jnp.concatenate(
            [
                jnp.concatenate(
                    [
                        x[q * frame : (q + 1) * frame, p * frame : (p + 1) * frame]
                        for q in range(slots)
                    ],
                    axis=1,
                )
                for p in range(2)
            ],
            axis=0,
        ).astype(dtype)

    ahead = tab[0]
    behind = tab[1]
    section = side_by_side(dot(waves[...], ahead))
    spectrum = dot(behind, section)
    p_re = probe[0].astype(F32)
    p_im = probe[1].astype(F32)
    residuals = []
    for quota in range(slots):
        s_re = spectrum[:frame, quota * frame : (quota + 1) * frame]
        s_im = spectrum[frame:, quota * frame : (quota + 1) * frame]
        magnitude = jnp.maximum(jnp.sqrt(s_re * s_re + s_im * s_im), 1.0)
        factor = (1.0 - levels[quota].astype(F32) / magnitude) * alive[quota, :1, :1]
        residuals.append(jnp.concatenate([s_re * factor, s_im * factor], axis=1).astype(BF))
    inverse = side_by_side(dot(jnp.concatenate(residuals, axis=0), behind))
    wave = dot(ahead, inverse)
    for quota in range(slots):
        b_re = wave[:frame, quota * frame : (quota + 1) * frame]
        b_im = wave[frame:, quota * frame : (quota + 1) * frame]
        back = jnp.concatenate(
            [p_re * b_re + p_im * b_im, p_re * b_im - p_im * b_re], axis=1
        ).astype(BF)
        cut = dot(picks[quota], back).astype(BF)
        for place, out in enumerate(outs):
            rows = cut[place * window : (place + 1) * window]
            held = out.shape[0]
            if held == slots:
                out[quota, 0] = rows[:, :frame]
                out[quota, 1] = rows[:, frame:]
                continue

            @pl.when(depth == quota // held)
            def _():
                out[quota % held, 0] = rows[:, :frame]
                out[quota % held, 1] = rows[:, frame:]


def place_kernel(strips, slots, share, rounds, laps, *refs):
    tables, refs = refs[:laps], refs[laps:]
    strip = lax.axis_index("strip")
    depth = lax.axis_index("depth")
    for (items, layers), left, columns in zip(rounds, refs[::2], refs[1::2]):
        _, frame, ny = columns.shape
        window = left.shape[1] // columns.shape[0]
        entry = 0
        for lap, kind, held in items:
            ints = Table(tables[lap], strips, slots, layers)
            reach = (2 * depth, 2 - 2 * depth, 1, 1)[kind]
            home = clip(strip - reach, strips - 1)
            for place in range(held):
                quota = place
                if held < slots:
                    quota = place + held * (depth if kind == 2 else 1 - depth)
                slot = ints.slot(home, quota)
                for z, shear in enumerate(ints.shears(home, slot)):
                    left[z * share : (z + 1) * share, entry * window : (entry + 1) * window] = (
                        band_matrix(share, window, MAX_SHEAR - shear)
                    )
                columns[entry] = band_matrix(frame, ny, ints.column(home, slot))
                entry += 1


def deposit_kernel(before, last, scale, left, columns, *refs):
    refs, total, sems = (refs[:-2], *refs[-2:]) if last else (refs, refs[-1], None)
    refs, out = refs[:-1], refs[-1]
    blocks, sums = (refs[:-1], refs[-1]) if before else (refs, None)
    layers, _, share, ny = out.shape
    window = blocks[0].shape[2]
    values = ([], [])
    entry = 0
    for block in blocks:
        for place in range(block.shape[0]):
            both = jnp.concatenate([block[place, 0], block[place, 1]], axis=0)
            placed = dot(both, columns[entry]).astype(BF)
            values[0].append(placed[:window])
            values[1].append(placed[window:])
            entry += 1
    left = left[...]
    copies = []
    for part in range(2):
        grown = dot(left, jnp.concatenate(values[part], axis=0)) * scale
        for z in range(layers):
            piece = grown[z * share : (z + 1) * share]
            total[z, part] = piece if sums is None else piece + sums[z, part]
            if last:
                copies.append(
                    pltpu.make_async_copy(total.at[z, part], out.at[z, part], sems.at[z, part])
                )
                copies[-1].start()
    for copy in copies:
        copy.wait()


def body(mesh_shape, crystal, probe, amplitude, shear, scan_x, scan_y, slot_angle, owner_slot, counts):
    strips, angles, depths = (mesh_shape[n] for n in ("strip", "angle", "depth"))
    slots = owner_slot.shape[2]
    quarter = strips // 4
    lanes = slots // quarter
    layers, _, wx, ny = crystal.shape
    frame = probe.shape[-1]
    share = wx // angles
    window = share + MAX_SHEAR
    half = amplitude.shape[1]
    axes = ("strip", "angle", "depth")
    params = pltpu.CompilerParams(vmem_limit_bytes=VMEM_BYTES)
    smem = pl.BlockSpec(memory_space=pltpu.SMEM)
    vmem = pl.BlockSpec(memory_space=pltpu.VMEM)

    def cost(micros):
        return pl.CostEstimate(flops=int(micros * 8e8), bytes_accessed=0, transcendentals=0)

    def swap(x):
        return lax.ppermute(x, "depth", [(d, (d + 1) % depths) for d in range(depths)])

    def permute(x, move):
        pairs = []
        for s in range(strips):
            for a in range(angles):
                for d in range(depths):
                    to = move(s, a, d)
                    if to is not None:
                        pairs.append(
                            (
                                (s * angles + a) * depths + d,
                                (to[0] * angles + to[1]) * depths + to[2],
                            )
                        )
        return lax.ppermute(x, axes, pairs)

    def ring(x, turn, lap):
        def move(s, a, d):
            way = turn if d == 0 else -turn
            if 0 <= s + way < strips:
                return s + way, (a + lap) % angles, d
            return s, a, 1 - d

        return permute(x, move)

    def far(x, way, lap, hops, forward):
        def move(s, a, d):
            reach = 2 * d if way else 1
            home = s - reach if forward else (s - 1 - 4 * hops) % strips
            if not 0 <= home <= strips - 3:
                return None
            to = (home + 1 + 4 * hops) % strips if forward else home + reach
            return to, (a + lap) % angles, d

        return permute(x, move)

    amplitude_far = swap(amplitude)
    by_slot = [jnp.swapaxes(x, 1, 2) for x in (scan_x, scan_y, slot_angle, owner_slot)]
    sources = (shear, *by_slot, counts)
    entries = shear.shape[0] * layers + 4 * strips * slots + strips
    table = pl.pallas_call(
        fill_kernel,
        out_shape=jax.ShapeDtypeStruct((entries,), jnp.int32),
        in_specs=[smem] * 6,
        out_specs=smem,
        compiler_params=pltpu.CompilerParams(vmem_limit_bytes=FILL_VMEM_BYTES),
        cost_estimate=cost(3),
        name="fill",
    )(*sources)
    tables = [table] + [
        lax.ppermute(table, "angle", [(a, (a + t) % angles) for a in range(angles)])
        for t in range(1, angles)
    ]
    sent = pl.pallas_call(
        functools.partial(project_kernel, strips, slots, False),
        out_shape=jax.ShapeDtypeStruct((slots, 2, half, frame), BF),
        in_specs=[smem, vmem],
        out_specs=vmem,
        compiler_params=params,
        cost_estimate=cost(1.5),
        name="project_far",
    )(table, crystal)
    arrived = swap(sent)
    moving, middle = pl.pallas_call(
        functools.partial(project_kernel, strips, slots, True),
        out_shape=[
            jax.ShapeDtypeStruct((slots, 2, half, frame), F32),
            jax.ShapeDtypeStruct((slots, 2, frame, frame), BF),
        ],
        in_specs=[smem, vmem],
        out_specs=[vmem, vmem],
        compiler_params=params,
        cost_estimate=cost(2.5),
        name="project_near",
    )(table, crystal)
    moving = pl.pallas_call(
        add_kernel,
        out_shape=jax.ShapeDtypeStruct(moving.shape, BF),
        in_specs=[vmem] * 2,
        out_specs=vmem,
        compiler_params=params,
        cost_estimate=cost(0.5),
        name="add",
    )(moving, arrived)

    moving, middle_table = lax.optimization_barrier((moving, table))

    def by_hops(x, near, beyond):
        if quarter == 1:
            return near(x)
        pieces = []
        for hops in range(quarter):
            piece = x[hops::quarter]
            pieces.append(near(piece) if hops == 0 else beyond(piece, hops))
        return jnp.stack(pieces, axis=1).reshape(x.shape)

    moved = by_hops(moving, lambda x: ring(x, 1, 0), lambda x, n: far(x, 1, 0, n, True))
    middle = by_hops(middle, lambda x: x, lambda x, n: far(x, 0, 0, n, True))
    middle_far = swap(middle)
    picks, alive = pl.pallas_call(
        functools.partial(cut_kernel, strips, angles, slots, layers, window),
        out_shape=[
            jax.ShapeDtypeStruct((slots, 2 * angles * window, frame), BF),
            jax.ShapeDtypeStruct((slots, 8, 128), F32),
        ],
        in_specs=[smem],
        out_specs=[vmem] * 2,
        compiler_params=params,
        cost_estimate=cost(0.5),
        name="cut",
    )(middle_table)
    moved, tables, amplitude_far, picks, alive = lax.optimization_barrier(
        (moved, tables, amplitude_far, picks, alive)
    )
    moved_far = swap(moved)
    split = quarter == 1 and slots % depths == 0
    held = slots // depths if split else slots
    cuts = pl.pallas_call(
        functools.partial(transform_kernel, angles, slots, window),
        out_shape=[
            jax.ShapeDtypeStruct((held if i > 1 and i % 2 else slots, 2, window, frame), BF)
            for i in range(2 * angles)
        ],
        in_specs=[vmem] * 10,
        out_specs=[vmem] * (2 * angles),
        scratch_shapes=[
            pltpu.VMEM((slots * frame, 2 * frame), BF),
            pltpu.VMEM((slots, frame, frame), BF),
        ],
        compiler_params=params,
        cost_estimate=cost(3),
        name="transform",
    )(
        moved, moved_far, middle, middle_far,
        amplitude, amplitude_far, probe, jnp.asarray(dft_tables(frame)),
        picks, alive,
    )
    *cuts, tables = lax.optimization_barrier([*cuts, tables])
    blocks = {}
    for lap in reversed(range(angles)):
        blocks[lap, 0] = by_hops(
            cuts[2 * lap],
            lambda x: ring(x, -1, lap),
            lambda x, n: far(x, 1, lap, n, False),
        )
        blocks[lap, 2] = by_hops(
            cuts[2 * lap + 1],
            lambda x: x
            if lap == 0
            else lax.ppermute(x, "angle", [(a, (a + lap) % angles) for a in range(angles)]),
            lambda x, n: far(x, 0, lap, n, False),
        )
    scale = 1.0 / (shear.shape[0] * angles)

    later = range(1, angles)
    keys = [(lap, kind) for lap in later for kind in (0, 2)] + [(0, 0)]
    shared = {0: 1, 2: 3} if split else {0: 1}
    rounds = [
        [(lap, kind, blocks[lap, kind].shape[0]) for lap, kind in keys + [(0, 2)]],
        [(lap, shared[kind], blocks[lap, kind].shape[0]) for lap, kind in keys if kind in shared],
    ]
    shapes = []
    for items in rounds:
        entries = sum(held for _, _, held in items)
        shapes.append(jax.ShapeDtypeStruct((layers * share, entries * window), BF))
        shapes.append(jax.ShapeDtypeStruct((entries, frame, ny), BF))
    places = pl.pallas_call(
        functools.partial(
            place_kernel, strips, slots, share, [(items, layers) for items in rounds], angles
        ),
        out_shape=shapes,
        in_specs=[smem] * angles,
        out_specs=[vmem] * len(shapes),
        compiler_params=params,
        cost_estimate=cost(1.5),
        name="place",
    )(*tables)
    arrivals = lax.optimization_barrier([blocks[key] for key in keys] + list(places))
    blocks.update(zip(keys, arrivals))
    places = arrivals[len(keys) :]
    others = [(lap, shared[kind]) for lap, kind in keys if kind in shared]
    own = keys + [(0, 2)]
    blocks.update({(lap, shared[kind]): swap(blocks[lap, kind]) for lap, kind in keys if kind in shared})

    def deposit(items, places, sums, last):
        sums = [] if sums is None else [sums]
        shape = (layers, 2, share, ny)
        return pl.pallas_call(
            functools.partial(deposit_kernel, bool(sums), last, scale),
            out_shape=jax.ShapeDtypeStruct(shape, F32),
            in_specs=[vmem] * (2 + len(items) + len(sums)),
            out_specs=pl.BlockSpec(memory_space=pltpu.HBM) if last else vmem,
            scratch_shapes=[pltpu.VMEM(shape, F32), pltpu.SemaphoreType.DMA((layers, 2))]
            if last
            else [],
            compiler_params=params,
            cost_estimate=cost(0.05),
            name="deposit",
        )(*places, *(blocks[item] for item in items), *sums)

    return deposit(others, places[2:], deposit(own, places[:2], None, False), True)


def solution(mesh):
    placed = (
        P(("groups", "depth"), None, "strip", None),
        P(),
        P("angle", ("groups", "strip", "depth"), None),
        P(("groups", "angle"), "depth"),
        P(("groups", "angle"), None, None),
        P(("groups", "angle"), None, None),
        P(("groups", "angle"), None, None),
        P(("groups", "angle"), None, None),
        P(("groups", "angle"), None),
    )
    return jax.shard_map(
        functools.partial(body, dict(mesh.shape)),
        mesh=mesh,
        in_specs=placed,
        out_specs=P(("groups", "depth"), None, ("strip", "angle"), None),
        check_vma=False,
    )
```

```python
import functools
import math

import jax
import jax.numpy as jnp
import ml_dtypes
import numpy as np
from jax import lax
from jax.experimental import pallas as pl
from jax.experimental.pallas import tpu as pltpu
from jax.sharding import PartitionSpec as P

BF = jnp.bfloat16
F32 = jnp.float32
VMEM_BYTES = 48 * 2**20
FILL_VMEM_BYTES = 54 * 2**20
MAX_SHEAR = 16


def dft_tables(n):
    index = np.arange(n, dtype=np.int64)
    phase = (index[:, None] * index[None, :] % n).astype(np.float64) * (2.0 * math.pi / n)
    scale = 1.0 / math.sqrt(n)
    re, im = np.cos(phase) * scale, -np.sin(phase) * scale
    tables = np.stack([np.block([[re, im], [-im, re]]), np.block([[re, -im], [im, re]])])
    return tables.astype(np.float32).astype(ml_dtypes.bfloat16)


def dot(left, right):
    return jnp.dot(left, right, preferred_element_type=F32)


def band_matrix(rows, cols, offset):
    gap = lax.broadcasted_iota(jnp.int32, (rows, cols), 1) - lax.broadcasted_iota(
        jnp.int32, (rows, cols), 0
    )
    return jnp.where(gap == offset, 1.0, 0.0).astype(BF)


def clip(value, top):
    return jnp.minimum(jnp.maximum(value, 0), top)


class Table:
    def __init__(self, ref, strips, slots, layers):
        self.ref, self.slots, self.layers = ref, slots, layers
        self.count = strips * slots
        self.base = ref.shape[0] - 4 * self.count - strips

    def pick(self, which, home, slot):
        return self.ref[self.base + which * self.count + home * self.slots + slot]

    def column(self, home, slot):
        return self.pick(0, home, slot)

    def shears(self, home, slot):
        angle = self.pick(1, home, slot)
        return [self.ref[angle * self.layers + z] for z in range(self.layers)]

    def slot(self, home, quota):
        found = jnp.int32(0)
        for slot in range(self.slots):
            found = jnp.where(self.pick(2, home, slot) == quota, slot, found)
        return found

    def offset(self, home, slot):
        return self.pick(3, home, slot)

    def alive(self, home, slot):
        return slot < self.ref[self.base + 4 * self.count + home]


def fill_kernel(shear, scan_x, scan_y, slot_angle, owner, counts, table):
    place = 0
    for i in range(shear.shape[0]):
        for z in range(shear.shape[1]):
            table[place] = shear[i, z]
            place += 1
    _, slots, strips = scan_x.shape
    for ref in (scan_y, slot_angle, owner, scan_x):
        for home in range(strips):
            for slot in range(slots):
                table[place] = ref[0, slot, home]
                place += 1
    for home in range(strips):
        table[place] = counts[0, home]
        place += 1


def project_kernel(strips, slots, mine, kinds, *refs):
    strip = lax.axis_index("strip")
    depth = lax.axis_index("depth")
    half = depth if mine else 1 - depth
    table, crystal, *parts = refs
    layers, _, wx, ny = crystal.shape
    ints = Table(table, strips, slots, layers)
    frame = parts[0].shape[-1]
    rows = []
    columns = []
    for kind, out in zip(kinds, parts):
        home = clip(strip - (2 * half if kind == 0 else 1), strips - 1)
        back = wx * (1 - half if kind == 1 else half)
        for quota in range(slots):
            slot = ints.slot(home, quota)
            start = ints.offset(home, slot) - back
            rows.append(
                jnp.concatenate(
                    [
                        band_matrix(out.shape[2], wx, start + shear)
                        for shear in ints.shears(home, slot)
                    ],
                    axis=1,
                )
            )
            columns.append(band_matrix(ny, frame, -ints.column(home, slot)))
    rows = jnp.concatenate(rows, axis=0)
    lifted = [
        dot(rows, jnp.concatenate([crystal[z, part] for z in range(layers)], axis=0)).astype(BF)
        for part in range(2)
    ]
    place = 0
    for entry, out in enumerate(parts):
        tall = out.shape[2]
        for quota in range(slots):
            both = jnp.concatenate([x[place : place + tall] for x in lifted], axis=0)
            band = dot(both, columns[entry * slots + quota]).astype(out.dtype)
            out[quota, 0] = band[:tall]
            out[quota, 1] = band[tall:]
            place += tall


def add_kernel(near, far, out):
    out[...] = (near[...] + far[...].astype(F32)).astype(out.dtype)


def cut_kernel(strips, angles, slots, layers, window, table, picks, alive):
    ints = Table(table, strips, slots, layers)
    quarter = strips // 4
    strip = lax.axis_index("strip")
    plane = lax.axis_index("angle")
    depth = lax.axis_index("depth")
    share = window - MAX_SHEAR
    for quota in range(slots):
        home = lax.rem(strip + (strips - 1) + 4 * (strips - quota % quarter), strips)
        slot = ints.slot(home, quota)
        live = jnp.logical_and(home <= strips - 3, ints.alive(home, slot))
        alive[quota] = jnp.full(alive.shape[1:], jnp.where(live, 1.0, 0.0), F32)
        offset = ints.offset(home, slot)
        for shift in range(angles):
            target = lax.rem(plane + shift, angles)
            for kind in range(2):
                reach = 2 * depth if kind == 0 else 1
                first = reach * (share * angles) + share * target - offset - MAX_SHEAR
                place = (2 * shift + kind) * window
                picks[quota, place : place + window] = band_matrix(window, picks.shape[2], first)


def section_kernel(moved, middle, middle_far, probe, tab, out, waves):
    slots, _, half, frame = moved.shape
    here = pl.ds(pl.multiple_of(lax.axis_index("depth") * half, half), half)
    p_re = probe[0, here].astype(F32)
    p_im = probe[1, here].astype(F32)
    for quota in range(slots):
        w_re, w_im = (
            moved[quota, part].astype(F32)
            + middle[quota, part].astype(F32)
            + middle_far[quota, part].astype(F32)
            for part in range(2)
        )
        to = slice(quota * half, (quota + 1) * half)
        waves[to, :frame] = (p_re * w_re - p_im * w_im).astype(BF)
        waves[to, frame:] = (p_re * w_im + p_im * w_re).astype(BF)
    out[...] = dot(waves[...], tab[0]).astype(BF)


def transform_kernel(angles, slots, window, *refs):
    section_near, section_far, near, far, probe, tab, picks, alive = refs[:8]
    outs = refs[8 : 8 + 2 * angles]
    sections, levels = refs[8 + 2 * angles :]
    depth = lax.axis_index("depth")
    half, frame = near.shape[1:]
    row = pl.multiple_of(depth * half, half)
    row_far = pl.multiple_of((1 - depth) * half, half)
    for quota in range(slots):
        levels[quota, pl.ds(row, half)] = near[quota]
        levels[quota, pl.ds(row_far, half)] = far[quota]

    def side_by_side(x, dtype=BF):
        return jnp.concatenate(
            [
                jnp.concatenate(
                    [
                        x[q * frame : (q + 1) * frame, p * frame : (p + 1) * frame]
                        for q in range(slots)
                    ],
                    axis=1,
                )
                for p in range(2)
            ],
            axis=0,
        ).astype(dtype)

    ahead = tab[0]
    behind = tab[1]
    for first, x in ((row, section_near), (row_far, section_far)):
        for quota in range(slots):
            for part in range(2):
                sections[
                    pl.ds(part * frame + first, half), quota * frame : (quota + 1) * frame
                ] = x[quota * half : (quota + 1) * half, part * frame : (part + 1) * frame]
    section = sections[...]
    spectrum = dot(behind, section)
    p_re = probe[0].astype(F32)
    p_im = probe[1].astype(F32)
    residuals = []
    for quota in range(slots):
        s_re = spectrum[:frame, quota * frame : (quota + 1) * frame]
        s_im = spectrum[frame:, quota * frame : (quota + 1) * frame]
        magnitude = jnp.maximum(jnp.sqrt(s_re * s_re + s_im * s_im), 1.0)
        factor = (1.0 - levels[quota].astype(F32) / magnitude) * alive[quota, :1, :1]
        residuals.append(jnp.concatenate([s_re * factor, s_im * factor], axis=1).astype(BF))
    inverse = side_by_side(dot(jnp.concatenate(residuals, axis=0), behind))
    wave = dot(ahead, inverse)
    for quota in range(slots):
        b_re = wave[:frame, quota * frame : (quota + 1) * frame]
        b_im = wave[frame:, quota * frame : (quota + 1) * frame]
        back = jnp.concatenate(
            [p_re * b_re + p_im * b_im, p_re * b_im - p_im * b_re], axis=1
        ).astype(BF)
        cut = dot(picks[quota], back).astype(BF)
        for place, out in enumerate(outs):
            rows = cut[place * window : (place + 1) * window]
            held = out.shape[0]
            if held == slots:
                out[quota, 0] = rows[:, :frame]
                out[quota, 1] = rows[:, frame:]
                continue

            @pl.when(depth == quota // held)
            def _():
                out[quota % held, 0] = rows[:, :frame]
                out[quota % held, 1] = rows[:, frame:]


def place_kernel(strips, slots, share, rounds, laps, *refs):
    tables, refs = refs[:laps], refs[laps:]
    strip = lax.axis_index("strip")
    depth = lax.axis_index("depth")
    for (items, layers), left, columns in zip(rounds, refs[::2], refs[1::2]):
        _, frame, ny = columns.shape
        window = left.shape[1] // columns.shape[0]
        entry = 0
        for lap, kind, held in items:
            ints = Table(tables[lap], strips, slots, layers)
            reach = (2 * depth, 2 - 2 * depth, 1, 1)[kind]
            home = clip(strip - reach, strips - 1)
            for place in range(held):
                quota = place
                if held < slots:
                    quota = place + held * (depth if kind == 2 else 1 - depth)
                slot = ints.slot(home, quota)
                for z, shear in enumerate(ints.shears(home, slot)):
                    left[z * share : (z + 1) * share, entry * window : (entry + 1) * window] = (
                        band_matrix(share, window, MAX_SHEAR - shear)
                    )
                columns[entry] = band_matrix(frame, ny, ints.column(home, slot))
                entry += 1


def deposit_kernel(before, last, scale, left, columns, *refs):
    refs, total, sems = (refs[:-2], *refs[-2:]) if last else (refs, refs[-1], None)
    refs, out = refs[:-1], refs[-1]
    blocks, sums = (refs[:-1], refs[-1]) if before else (refs, None)
    layers, _, share, ny = out.shape
    window = blocks[0].shape[2]
    values = ([], [])
    entry = 0
    for block in blocks:
        for place in range(block.shape[0]):
            both = jnp.concatenate([block[place, 0], block[place, 1]], axis=0)
            placed = dot(both, columns[entry]).astype(BF)
            values[0].append(placed[:window])
            values[1].append(placed[window:])
            entry += 1
    left = left[...]
    copies = []
    for part in range(2):
        grown = dot(left, jnp.concatenate(values[part], axis=0)) * scale
        for z in range(layers):
            piece = grown[z * share : (z + 1) * share]
            total[z, part] = piece if sums is None else piece + sums[z, part]
            if last:
                copies.append(
                    pltpu.make_async_copy(total.at[z, part], out.at[z, part], sems.at[z, part])
                )
                copies[-1].start()
    for copy in copies:
        copy.wait()


def body(mesh_shape, crystal, probe, amplitude, shear, scan_x, scan_y, slot_angle, owner_slot, counts):
    strips, angles, depths = (mesh_shape[n] for n in ("strip", "angle", "depth"))
    slots = owner_slot.shape[2]
    quarter = strips // 4
    lanes = slots // quarter
    layers, _, wx, ny = crystal.shape
    frame = probe.shape[-1]
    share = wx // angles
    window = share + MAX_SHEAR
    half = amplitude.shape[1]
    axes = ("strip", "angle", "depth")
    params = pltpu.CompilerParams(vmem_limit_bytes=VMEM_BYTES)
    smem = pl.BlockSpec(memory_space=pltpu.SMEM)
    vmem = pl.BlockSpec(memory_space=pltpu.VMEM)

    def cost(micros):
        return pl.CostEstimate(flops=int(micros * 8e8), bytes_accessed=0, transcendentals=0)

    def swap(x):
        return lax.ppermute(x, "depth", [(d, (d + 1) % depths) for d in range(depths)])

    def permute(x, move):
        pairs = []
        for s in range(strips):
            for a in range(angles):
                for d in range(depths):
                    to = move(s, a, d)
                    if to is not None:
                        pairs.append(
                            (
                                (s * angles + a) * depths + d,
                                (to[0] * angles + to[1]) * depths + to[2],
                            )
                        )
        return lax.ppermute(x, axes, pairs)

    def ring(x, turn, lap):
        def move(s, a, d):
            way = turn if d == 0 else -turn
            if 0 <= s + way < strips:
                return s + way, (a + lap) % angles, d
            return s, a, 1 - d

        return permute(x, move)

    def far(x, way, lap, hops, forward):
        def move(s, a, d):
            reach = 2 * d if way else 1
            home = s - reach if forward else (s - 1 - 4 * hops) % strips
            if not 0 <= home <= strips - 3:
                return None
            to = (home + 1 + 4 * hops) % strips if forward else home + reach
            return to, (a + lap) % angles, d

        return permute(x, move)

    amplitude_far = swap(amplitude)
    by_slot = [jnp.swapaxes(x, 1, 2) for x in (scan_x, scan_y, slot_angle, owner_slot)]
    sources = (shear, *by_slot, counts)
    entries = shear.shape[0] * layers + 4 * strips * slots + strips
    table = pl.pallas_call(
        fill_kernel,
        out_shape=jax.ShapeDtypeStruct((entries,), jnp.int32),
        in_specs=[smem] * 6,
        out_specs=smem,
        compiler_params=pltpu.CompilerParams(vmem_limit_bytes=FILL_VMEM_BYTES),
        cost_estimate=cost(3),
        name="fill",
    )(*sources)
    sent = pl.pallas_call(
        functools.partial(project_kernel, strips, slots, False, (0,)),
        out_shape=jax.ShapeDtypeStruct((slots, 2, half, frame), BF),
        in_specs=[smem, vmem],
        out_specs=vmem,
        compiler_params=params,
        cost_estimate=cost(1.5),
        name="project_far",
    )(table, crystal)
    arrived = swap(sent)

    def project(kinds, dtype, micros, name):
        return pl.pallas_call(
            functools.partial(project_kernel, strips, slots, True, kinds),
            out_shape=[jax.ShapeDtypeStruct((slots, 2, half, frame), dtype)] * len(kinds),
            in_specs=[smem, vmem],
            out_specs=[vmem] * len(kinds),
            compiler_params=params,
            cost_estimate=cost(micros),
            name=name,
        )

    (moving,) = project((0,), F32, 1.5, "project_near")(table, crystal)
    moving = pl.pallas_call(
        add_kernel,
        out_shape=jax.ShapeDtypeStruct(moving.shape, BF),
        in_specs=[vmem] * 2,
        out_specs=vmem,
        compiler_params=params,
        cost_estimate=cost(0.5),
        name="add",
    )(moving, arrived)

    moving, middle_table = lax.optimization_barrier((moving, table))
    middle, middle_sent = project((1, 2), BF, 1.5, "project_middle")(middle_table, crystal)

    def by_hops(x, near, beyond):
        if quarter == 1:
            return near(x)
        pieces = []
        for hops in range(quarter):
            piece = x[hops::quarter]
            pieces.append(near(piece) if hops == 0 else beyond(piece, hops))
        return jnp.stack(pieces, axis=1).reshape(x.shape)

    moved = by_hops(moving, lambda x: ring(x, 1, 0), lambda x, n: far(x, 1, 0, n, True))
    middle, middle_sent = (
        by_hops(x, lambda x: x, lambda x, n: far(x, 0, 0, n, True)) for x in (middle, middle_sent)
    )
    middle_far = swap(middle_sent)
    picks, alive = pl.pallas_call(
        functools.partial(cut_kernel, strips, angles, slots, layers, window),
        out_shape=[
            jax.ShapeDtypeStruct((slots, 2 * angles * window, frame), BF),
            jax.ShapeDtypeStruct((slots, 8, 128), F32),
        ],
        in_specs=[smem],
        out_specs=[vmem] * 2,
        compiler_params=params,
        cost_estimate=cost(0.5),
        name="cut",
    )(middle_table)
    moved, amplitude_far, picks, alive, table = lax.optimization_barrier(
        (moved, amplitude_far, picks, alive, middle_table)
    )
    tables = [table] + [
        lax.ppermute(table, "angle", [(a, (a + t) % angles) for a in range(angles)])
        for t in range(1, angles)
    ]
    tab = jnp.asarray(dft_tables(frame))
    section_near = pl.pallas_call(
        section_kernel,
        out_shape=jax.ShapeDtypeStruct((slots * half, 2 * frame), BF),
        in_specs=[vmem] * 5,
        out_specs=vmem,
        scratch_shapes=[pltpu.VMEM((slots * half, 2 * frame), BF)],
        compiler_params=params,
        cost_estimate=cost(0.7),
        name="section",
    )(moved, middle, middle_far, probe, tab)
    split = quarter == 1 and slots % depths == 0
    held = slots // depths if split else slots
    cuts = pl.pallas_call(
        functools.partial(transform_kernel, angles, slots, window),
        out_shape=[
            jax.ShapeDtypeStruct((held if i > 1 and i % 2 else slots, 2, window, frame), BF)
            for i in range(2 * angles)
        ],
        in_specs=[vmem] * 8,
        out_specs=[vmem] * (2 * angles),
        scratch_shapes=[
            pltpu.VMEM((2 * frame, slots * frame), BF),
            pltpu.VMEM((slots, frame, frame), BF),
        ],
        compiler_params=params,
        cost_estimate=cost(3),
        name="transform",
    )(
        section_near, swap(section_near),
        amplitude, amplitude_far, probe, tab,
        picks, alive,
    )
    *cuts, tables = lax.optimization_barrier([*cuts, tables])
    blocks = {}
    for lap in reversed(range(angles)):
        blocks[lap, 0] = by_hops(
            cuts[2 * lap],
            lambda x: ring(x, -1, lap),
            lambda x, n: far(x, 1, lap, n, False),
        )
        blocks[lap, 2] = by_hops(
            cuts[2 * lap + 1],
            lambda x: x
            if lap == 0
            else lax.ppermute(x, "angle", [(a, (a + lap) % angles) for a in range(angles)]),
            lambda x, n: far(x, 0, lap, n, False),
        )
    scale = 1.0 / (shear.shape[0] * angles)

    later = range(1, angles)
    keys = [(lap, kind) for lap in later for kind in (0, 2)] + [(0, 0)]
    shared = {0: 1, 2: 3} if split else {0: 1}
    rounds = [
        [(lap, kind, blocks[lap, kind].shape[0]) for lap, kind in keys + [(0, 2)]],
        [(lap, shared[kind], blocks[lap, kind].shape[0]) for lap, kind in keys if kind in shared],
    ]
    shapes = []
    for items in rounds:
        entries = sum(held for _, _, held in items)
        shapes.append(jax.ShapeDtypeStruct((layers * share, entries * window), BF))
        shapes.append(jax.ShapeDtypeStruct((entries, frame, ny), BF))
    places = pl.pallas_call(
        functools.partial(
            place_kernel, strips, slots, share, [(items, layers) for items in rounds], angles
        ),
        out_shape=shapes,
        in_specs=[smem] * angles,
        out_specs=[vmem] * len(shapes),
        compiler_params=params,
        cost_estimate=cost(1.5),
        name="place",
    )(*tables)
    arrivals = lax.optimization_barrier([blocks[key] for key in keys] + list(places))
    blocks.update(zip(keys, arrivals))
    places = arrivals[len(keys) :]
    others = [(lap, shared[kind]) for lap, kind in keys if kind in shared]
    own = keys + [(0, 2)]
    blocks.update({(lap, shared[kind]): swap(blocks[lap, kind]) for lap, kind in keys if kind in shared})

    def deposit(items, places, sums, last):
        sums = [] if sums is None else [sums]
        shape = (layers, 2, share, ny)
        return pl.pallas_call(
            functools.partial(deposit_kernel, bool(sums), last, scale),
            out_shape=jax.ShapeDtypeStruct(shape, F32),
            in_specs=[vmem] * (2 + len(items) + len(sums)),
            out_specs=pl.BlockSpec(memory_space=pltpu.HBM) if last else vmem,
            scratch_shapes=[pltpu.VMEM(shape, F32), pltpu.SemaphoreType.DMA((layers, 2))]
            if last
            else [],
            compiler_params=params,
            cost_estimate=cost(0.05),
            name="deposit",
        )(*places, *(blocks[item] for item in items), *sums)

    return deposit(others, places[2:], deposit(own, places[:2], None, False), True)


def solution(mesh):
    placed = (
        P(("groups", "depth"), None, "strip", None),
        P(),
        P("angle", ("groups", "strip", "depth"), None),
        P(("groups", "angle"), "depth"),
        P(("groups", "angle"), None, None),
        P(("groups", "angle"), None, None),
        P(("groups", "angle"), None, None),
        P(("groups", "angle"), None, None),
        P(("groups", "angle"), None),
    )
    return jax.shard_map(
        functools.partial(body, dict(mesh.shape)),
        mesh=mesh,
        in_specs=placed,
        out_specs=P(("groups", "depth"), None, ("strip", "angle"), None),
        check_vma=False,
    )
```

```python
import functools
import math

import jax
import jax.numpy as jnp
import ml_dtypes
import numpy as np
from jax import lax
from jax.experimental import pallas as pl
from jax.experimental.pallas import tpu as pltpu
from jax.sharding import PartitionSpec as P

BF = jnp.bfloat16
F32 = jnp.float32
VMEM_BYTES = 48 * 2**20
FILL_VMEM_BYTES = 54 * 2**20
MAX_SHEAR = 16


def dft_tables(n):
    index = np.arange(n, dtype=np.int64)
    phase = (index[:, None] * index[None, :] % n).astype(np.float64) * (2.0 * math.pi / n)
    scale = 1.0 / math.sqrt(n)
    re, im = np.cos(phase) * scale, -np.sin(phase) * scale
    tables = np.stack([np.block([[re, im], [-im, re]]), np.block([[re, -im], [im, re]])])
    return tables.astype(np.float32).astype(ml_dtypes.bfloat16)


def dot(left, right):
    return jnp.dot(left, right, preferred_element_type=F32)


def band_matrix(rows, cols, offset):
    gap = lax.broadcasted_iota(jnp.int32, (rows, cols), 1) - lax.broadcasted_iota(
        jnp.int32, (rows, cols), 0
    )
    return jnp.where(gap == offset, 1.0, 0.0).astype(BF)


def clip(value, top):
    return jnp.minimum(jnp.maximum(value, 0), top)


class Table:
    def __init__(self, ref, strips, slots, layers):
        self.ref, self.slots, self.layers = ref, slots, layers
        self.count = strips * slots
        self.base = ref.shape[0] - 4 * self.count - strips

    def pick(self, which, home, slot):
        return self.ref[self.base + which * self.count + home * self.slots + slot]

    def column(self, home, slot):
        return self.pick(0, home, slot)

    def shears(self, home, slot):
        angle = self.pick(1, home, slot)
        return [self.ref[angle * self.layers + z] for z in range(self.layers)]

    def slot(self, home, quota):
        found = jnp.int32(0)
        for slot in range(self.slots):
            found = jnp.where(self.pick(2, home, slot) == quota, slot, found)
        return found

    def offset(self, home, slot):
        return self.pick(3, home, slot)

    def alive(self, home, slot):
        return slot < self.ref[self.base + 4 * self.count + home]


def fill_kernel(shear, scan_x, scan_y, slot_angle, owner, counts, table):
    place = 0
    for i in range(shear.shape[0]):
        for z in range(shear.shape[1]):
            table[place] = shear[i, z]
            place += 1
    _, slots, strips = scan_x.shape
    for ref in (scan_y, slot_angle, owner, scan_x):
        for home in range(strips):
            for slot in range(slots):
                table[place] = ref[0, slot, home]
                place += 1
    for home in range(strips):
        table[place] = counts[0, home]
        place += 1


def project_kernel(strips, slots, mine, kinds, *refs):
    strip = lax.axis_index("strip")
    depth = lax.axis_index("depth")
    half = depth if mine else 1 - depth
    table, crystal, *parts = refs
    layers, _, wx, ny = crystal.shape
    ints = Table(table, strips, slots, layers)
    frame = parts[0].shape[-1]
    rows = []
    columns = []
    for kind, out in zip(kinds, parts):
        home = clip(strip - (2 * half if kind == 0 else 1), strips - 1)
        back = wx * (1 - half if kind == 1 else half)
        for quota in range(slots):
            slot = ints.slot(home, quota)
            start = ints.offset(home, slot) - back
            rows.append(
                jnp.concatenate(
                    [
                        band_matrix(out.shape[2], wx, start + shear)
                        for shear in ints.shears(home, slot)
                    ],
                    axis=1,
                )
            )
            columns.append(band_matrix(ny, frame, -ints.column(home, slot)))
    rows = jnp.concatenate(rows, axis=0)
    lifted = [
        dot(rows, jnp.concatenate([crystal[z, part] for z in range(layers)], axis=0)).astype(BF)
        for part in range(2)
    ]
    place = 0
    for entry, out in enumerate(parts):
        tall = out.shape[2]
        for quota in range(slots):
            both = jnp.concatenate([x[place : place + tall] for x in lifted], axis=0)
            band = dot(both, columns[entry * slots + quota]).astype(out.dtype)
            out[quota, 0] = band[:tall]
            out[quota, 1] = band[tall:]
            place += tall


def add_kernel(near, far, out):
    out[...] = (near[...] + far[...].astype(F32)).astype(out.dtype)


def cut_kernel(strips, angles, slots, layers, window, table, picks, alive):
    ints = Table(table, strips, slots, layers)
    quarter = strips // 4
    strip = lax.axis_index("strip")
    plane = lax.axis_index("angle")
    depth = lax.axis_index("depth")
    share = window - MAX_SHEAR
    for quota in range(slots):
        home = lax.rem(strip + (strips - 1) + 4 * (strips - quota % quarter), strips)
        slot = ints.slot(home, quota)
        live = jnp.logical_and(home <= strips - 3, ints.alive(home, slot))
        alive[quota] = jnp.full(alive.shape[1:], jnp.where(live, 1.0, 0.0), F32)
        offset = ints.offset(home, slot)
        for shift in range(angles):
            target = lax.rem(plane + shift, angles)
            for kind in range(2):
                reach = 2 * depth if kind == 0 else 1
                first = reach * (share * angles) + share * target - offset - MAX_SHEAR
                place = (2 * shift + kind) * window
                picks[quota, place : place + window] = band_matrix(window, picks.shape[2], first)


def section_kernel(moved, middle, middle_far, probe, tab, out, waves):
    slots, _, half, frame = moved.shape
    here = pl.ds(pl.multiple_of(lax.axis_index("depth") * half, half), half)
    p_re = probe[0, here].astype(F32)
    p_im = probe[1, here].astype(F32)
    for quota in range(slots):
        w_re, w_im = (
            moved[quota, part].astype(F32)
            + middle[quota, part].astype(F32)
            + middle_far[quota, part].astype(F32)
            for part in range(2)
        )
        to = slice(quota * half, (quota + 1) * half)
        waves[to, :frame] = (p_re * w_re - p_im * w_im).astype(BF)
        waves[to, frame:] = (p_re * w_im + p_im * w_re).astype(BF)
    out[...] = dot(waves[...], tab[0]).astype(BF)


def transform_kernel(angles, slots, window, *refs):
    section_near, section_far, near, far, probe, tab, picks, alive = refs[:8]
    outs = refs[8 : 8 + 2 * angles]
    sections, levels = refs[8 + 2 * angles :]
    depth = lax.axis_index("depth")
    half, frame = near.shape[1:]
    row = pl.multiple_of(depth * half, half)
    row_far = pl.multiple_of((1 - depth) * half, half)
    for quota in range(slots):
        levels[quota, pl.ds(row, half)] = near[quota]
        levels[quota, pl.ds(row_far, half)] = far[quota]

    def side_by_side(x, dtype=BF):
        return jnp.concatenate(
            [
                jnp.concatenate(
                    [
                        x[q * frame : (q + 1) * frame, p * frame : (p + 1) * frame]
                        for q in range(slots)
                    ],
                    axis=1,
                )
                for p in range(2)
            ],
            axis=0,
        ).astype(dtype)

    ahead = tab[0]
    behind = tab[1]
    for first, x in ((row, section_near), (row_far, section_far)):
        for quota in range(slots):
            for part in range(2):
                sections[
                    pl.ds(part * frame + first, half), quota * frame : (quota + 1) * frame
                ] = x[quota * half : (quota + 1) * half, part * frame : (part + 1) * frame]
    section = sections[...]
    spectrum = dot(behind, section)
    p_re = probe[0].astype(F32)
    p_im = probe[1].astype(F32)
    residuals = []
    for quota in range(slots):
        s_re = spectrum[:frame, quota * frame : (quota + 1) * frame]
        s_im = spectrum[frame:, quota * frame : (quota + 1) * frame]
        inverse_size = jnp.minimum(lax.rsqrt(s_re * s_re + s_im * s_im), 1.0)
        factor = (1.0 - levels[quota].astype(F32) * inverse_size) * alive[quota, :1, :1]
        residuals.append(jnp.concatenate([s_re * factor, s_im * factor], axis=1).astype(BF))
    inverse = side_by_side(dot(jnp.concatenate(residuals, axis=0), behind))
    wave = dot(ahead, inverse)
    for quota in range(slots):
        b_re = wave[:frame, quota * frame : (quota + 1) * frame]
        b_im = wave[frame:, quota * frame : (quota + 1) * frame]
        back = jnp.concatenate(
            [p_re * b_re + p_im * b_im, p_re * b_im - p_im * b_re], axis=1
        ).astype(BF)
        cut = dot(picks[quota], back).astype(BF)
        for place, out in enumerate(outs):
            rows = cut[place * window : (place + 1) * window]
            held = out.shape[0]
            if held == slots:
                out[quota, 0] = rows[:, :frame]
                out[quota, 1] = rows[:, frame:]
                continue

            @pl.when(depth == quota // held)
            def _():
                out[quota % held, 0] = rows[:, :frame]
                out[quota % held, 1] = rows[:, frame:]


def place_kernel(strips, slots, share, rounds, laps, *refs):
    tables, refs = refs[:laps], refs[laps:]
    strip = lax.axis_index("strip")
    depth = lax.axis_index("depth")
    for (items, layers), left, columns in zip(rounds, refs[::2], refs[1::2]):
        _, frame, ny = columns.shape
        window = left.shape[1] // columns.shape[0]
        entry = 0
        for lap, kind, held in items:
            ints = Table(tables[lap], strips, slots, layers)
            reach = (2 * depth, 2 - 2 * depth, 1, 1)[kind]
            home = clip(strip - reach, strips - 1)
            for place in range(held):
                quota = place
                if held < slots:
                    quota = place + held * (depth if kind == 2 else 1 - depth)
                slot = ints.slot(home, quota)
                for z, shear in enumerate(ints.shears(home, slot)):
                    left[z * share : (z + 1) * share, entry * window : (entry + 1) * window] = (
                        band_matrix(share, window, MAX_SHEAR - shear)
                    )
                columns[entry] = band_matrix(frame, ny, ints.column(home, slot))
                entry += 1


def deposit_kernel(before, last, scale, left, columns, *refs):
    refs, total, sems = (refs[:-2], *refs[-2:]) if last else (refs, refs[-1], None)
    refs, out = refs[:-1], refs[-1]
    blocks, sums = (refs[:-1], refs[-1]) if before else (refs, None)
    layers, _, share, ny = out.shape
    window = blocks[0].shape[2]
    values = ([], [])
    entry = 0
    for block in blocks:
        for place in range(block.shape[0]):
            both = jnp.concatenate([block[place, 0], block[place, 1]], axis=0)
            placed = dot(both, columns[entry]).astype(BF)
            values[0].append(placed[:window])
            values[1].append(placed[window:])
            entry += 1
    left = left[...]
    copies = []
    for part in range(2):
        grown = dot(left, jnp.concatenate(values[part], axis=0))
        for z in range(layers):
            piece = grown[z * share : (z + 1) * share]
            if before:
                piece = piece + sums[z, part]
            total[z, part] = piece * scale if last else piece
            if last:
                copies.append(
                    pltpu.make_async_copy(total.at[z, part], out.at[z, part], sems.at[z, part])
                )
                copies[-1].start()
    for copy in copies:
        copy.wait()


def body(mesh_shape, crystal, probe, amplitude, shear, scan_x, scan_y, slot_angle, owner_slot, counts):
    strips, angles, depths = (mesh_shape[n] for n in ("strip", "angle", "depth"))
    slots = owner_slot.shape[2]
    quarter = strips // 4
    lanes = slots // quarter
    layers, _, wx, ny = crystal.shape
    frame = probe.shape[-1]
    share = wx // angles
    window = share + MAX_SHEAR
    half = amplitude.shape[1]
    axes = ("strip", "angle", "depth")
    params = pltpu.CompilerParams(vmem_limit_bytes=VMEM_BYTES)
    smem = pl.BlockSpec(memory_space=pltpu.SMEM)
    vmem = pl.BlockSpec(memory_space=pltpu.VMEM)

    def cost(micros):
        return pl.CostEstimate(flops=int(micros * 8e8), bytes_accessed=0, transcendentals=0)

    def swap(x):
        return lax.ppermute(x, "depth", [(d, (d + 1) % depths) for d in range(depths)])

    def permute(x, move):
        pairs = []
        for s in range(strips):
            for a in range(angles):
                for d in range(depths):
                    to = move(s, a, d)
                    if to is not None:
                        pairs.append(
                            (
                                (s * angles + a) * depths + d,
                                (to[0] * angles + to[1]) * depths + to[2],
                            )
                        )
        return lax.ppermute(x, axes, pairs)

    def ring(x, turn, lap):
        def move(s, a, d):
            way = turn if d == 0 else -turn
            if 0 <= s + way < strips:
                return s + way, (a + lap) % angles, d
            return s, a, 1 - d

        return permute(x, move)

    def far(x, way, lap, hops, forward):
        def move(s, a, d):
            reach = 2 * d if way else 1
            home = s - reach if forward else (s - 1 - 4 * hops) % strips
            if not 0 <= home <= strips - 3:
                return None
            to = (home + 1 + 4 * hops) % strips if forward else home + reach
            return to, (a + lap) % angles, d

        return permute(x, move)

    amplitude_far = swap(amplitude)
    by_slot = [jnp.swapaxes(x, 1, 2) for x in (scan_x, scan_y, slot_angle, owner_slot)]
    sources = (shear, *by_slot, counts)
    entries = shear.shape[0] * layers + 4 * strips * slots + strips
    table = pl.pallas_call(
        fill_kernel,
        out_shape=jax.ShapeDtypeStruct((entries,), jnp.int32),
        in_specs=[smem] * 6,
        out_specs=smem,
        compiler_params=pltpu.CompilerParams(vmem_limit_bytes=FILL_VMEM_BYTES),
        cost_estimate=cost(3),
        name="fill",
    )(*sources)
    sent = pl.pallas_call(
        functools.partial(project_kernel, strips, slots, False, (0,)),
        out_shape=jax.ShapeDtypeStruct((slots, 2, half, frame), BF),
        in_specs=[smem, vmem],
        out_specs=vmem,
        compiler_params=params,
        cost_estimate=cost(1.5),
        name="project_far",
    )(table, crystal)
    arrived = swap(sent)

    def project(kinds, dtype, micros, name):
        return pl.pallas_call(
            functools.partial(project_kernel, strips, slots, True, kinds),
            out_shape=[jax.ShapeDtypeStruct((slots, 2, half, frame), dtype)] * len(kinds),
            in_specs=[smem, vmem],
            out_specs=[vmem] * len(kinds),
            compiler_params=params,
            cost_estimate=cost(micros),
            name=name,
        )

    (moving,) = project((0,), F32, 1.5, "project_near")(table, crystal)
    moving = pl.pallas_call(
        add_kernel,
        out_shape=jax.ShapeDtypeStruct(moving.shape, BF),
        in_specs=[vmem] * 2,
        out_specs=vmem,
        compiler_params=params,
        cost_estimate=cost(0.5),
        name="add",
    )(moving, arrived)

    moving, middle_table = lax.optimization_barrier((moving, table))
    middle, middle_sent = project((1, 2), BF, 1.5, "project_middle")(middle_table, crystal)

    def by_hops(x, near, beyond):
        if quarter == 1:
            return near(x)
        pieces = []
        for hops in range(quarter):
            piece = x[hops::quarter]
            pieces.append(near(piece) if hops == 0 else beyond(piece, hops))
        return jnp.stack(pieces, axis=1).reshape(x.shape)

    moved = by_hops(moving, lambda x: ring(x, 1, 0), lambda x, n: far(x, 1, 0, n, True))
    middle, middle_sent = (
        by_hops(x, lambda x: x, lambda x, n: far(x, 0, 0, n, True)) for x in (middle, middle_sent)
    )
    middle_far = swap(middle_sent)
    picks, alive = pl.pallas_call(
        functools.partial(cut_kernel, strips, angles, slots, layers, window),
        out_shape=[
            jax.ShapeDtypeStruct((slots, 2 * angles * window, frame), BF),
            jax.ShapeDtypeStruct((slots, 8, 128), F32),
        ],
        in_specs=[smem],
        out_specs=[vmem] * 2,
        compiler_params=params,
        cost_estimate=cost(0.5),
        name="cut",
    )(middle_table)
    moved, amplitude_far, picks, alive, table = lax.optimization_barrier(
        (moved, amplitude_far, picks, alive, middle_table)
    )
    tables = [table] + [
        lax.ppermute(table, "angle", [(a, (a + t) % angles) for a in range(angles)])
        for t in range(1, angles)
    ]
    tab = jnp.asarray(dft_tables(frame))
    section_near = pl.pallas_call(
        section_kernel,
        out_shape=jax.ShapeDtypeStruct((slots * half, 2 * frame), BF),
        in_specs=[vmem] * 5,
        out_specs=vmem,
        scratch_shapes=[pltpu.VMEM((slots * half, 2 * frame), BF)],
        compiler_params=params,
        cost_estimate=cost(0.7),
        name="section",
    )(moved, middle, middle_far, probe, tab)
    split = quarter == 1 and slots % depths == 0
    held = slots // depths if split else slots
    cuts = pl.pallas_call(
        functools.partial(transform_kernel, angles, slots, window),
        out_shape=[
            jax.ShapeDtypeStruct((held if i > 1 and i % 2 else slots, 2, window, frame), BF)
            for i in range(2 * angles)
        ],
        in_specs=[vmem] * 8,
        out_specs=[vmem] * (2 * angles),
        scratch_shapes=[
            pltpu.VMEM((2 * frame, slots * frame), BF),
            pltpu.VMEM((slots, frame, frame), BF),
        ],
        compiler_params=params,
        cost_estimate=cost(3),
        name="transform",
    )(
        section_near, swap(section_near),
        amplitude, amplitude_far, probe, tab,
        picks, alive,
    )
    *cuts, tables = lax.optimization_barrier([*cuts, tables])
    blocks = {}
    for lap in reversed(range(angles)):
        blocks[lap, 0] = by_hops(
            cuts[2 * lap],
            lambda x: ring(x, -1, lap),
            lambda x, n: far(x, 1, lap, n, False),
        )
        blocks[lap, 2] = by_hops(
            cuts[2 * lap + 1],
            lambda x: x
            if lap == 0
            else lax.ppermute(x, "angle", [(a, (a + lap) % angles) for a in range(angles)]),
            lambda x, n: far(x, 0, lap, n, False),
        )
    scale = 1.0 / (shear.shape[0] * angles)

    later = range(1, angles)
    keys = [(lap, kind) for lap in later for kind in (0, 2)] + [(0, 0)]
    shared = {0: 1, 2: 3} if split else {0: 1}
    rounds = [
        [(lap, kind, blocks[lap, kind].shape[0]) for lap, kind in keys + [(0, 2)]],
        [(lap, shared[kind], blocks[lap, kind].shape[0]) for lap, kind in keys if kind in shared],
    ]
    shapes = []
    for items in rounds:
        entries = sum(held for _, _, held in items)
        shapes.append(jax.ShapeDtypeStruct((layers * share, entries * window), BF))
        shapes.append(jax.ShapeDtypeStruct((entries, frame, ny), BF))
    places = pl.pallas_call(
        functools.partial(
            place_kernel, strips, slots, share, [(items, layers) for items in rounds], angles
        ),
        out_shape=shapes,
        in_specs=[smem] * angles,
        out_specs=[vmem] * len(shapes),
        compiler_params=params,
        cost_estimate=cost(1.5),
        name="place",
    )(*tables)
    arrivals = lax.optimization_barrier([blocks[key] for key in keys] + list(places))
    blocks.update(zip(keys, arrivals))
    places = arrivals[len(keys) :]
    others = [(lap, shared[kind]) for lap, kind in keys if kind in shared]
    own = keys + [(0, 2)]
    blocks.update({(lap, shared[kind]): swap(blocks[lap, kind]) for lap, kind in keys if kind in shared})

    def deposit(items, places, sums, last):
        sums = [] if sums is None else [sums]
        shape = (layers, 2, share, ny)
        return pl.pallas_call(
            functools.partial(deposit_kernel, bool(sums), last, scale),
            out_shape=jax.ShapeDtypeStruct(shape, F32),
            in_specs=[vmem] * (2 + len(items) + len(sums)),
            out_specs=pl.BlockSpec(memory_space=pltpu.HBM) if last else vmem,
            scratch_shapes=[pltpu.VMEM(shape, F32), pltpu.SemaphoreType.DMA((layers, 2))]
            if last
            else [],
            compiler_params=params,
            cost_estimate=cost(0.05),
            name="deposit",
        )(*places, *(blocks[item] for item in items), *sums)

    return deposit(others, places[2:], deposit(own, places[:2], None, False), True)


def solution(mesh):
    placed = (
        P(("groups", "depth"), None, "strip", None),
        P(),
        P("angle", ("groups", "strip", "depth"), None),
        P(("groups", "angle"), "depth"),
        P(("groups", "angle"), None, None),
        P(("groups", "angle"), None, None),
        P(("groups", "angle"), None, None),
        P(("groups", "angle"), None, None),
        P(("groups", "angle"), None),
    )
    return jax.shard_map(
        functools.partial(body, dict(mesh.shape)),
        mesh=mesh,
        in_specs=placed,
        out_specs=P(("groups", "depth"), None, ("strip", "angle"), None),
        check_vma=False,
    )
```

```python
import functools
import math

import jax
import jax.numpy as jnp
import ml_dtypes
import numpy as np
from jax import lax
from jax.experimental import pallas as pl
from jax.experimental.pallas import tpu as pltpu
from jax.sharding import PartitionSpec as P

BF = jnp.bfloat16
F32 = jnp.float32
VMEM_BYTES = 48 * 2**20
FILL_VMEM_BYTES = 54 * 2**20
MAX_SHEAR = 16


def dft_tables(n):
    index = np.arange(n, dtype=np.int64)
    phase = (index[:, None] * index[None, :] % n).astype(np.float64) * (2.0 * math.pi / n)
    scale = 1.0 / math.sqrt(n)
    re, im = np.cos(phase) * scale, -np.sin(phase) * scale
    tables = np.stack([np.block([[re, im], [-im, re]]), np.block([[re, -im], [im, re]])])
    return tables.astype(np.float32).astype(ml_dtypes.bfloat16)


def dot(left, right):
    return jnp.dot(left, right, preferred_element_type=F32)


def band_matrix(rows, cols, offset):
    gap = lax.broadcasted_iota(jnp.int32, (rows, cols), 1) - lax.broadcasted_iota(
        jnp.int32, (rows, cols), 0
    )
    return jnp.where(gap == offset, 1.0, 0.0).astype(BF)


def clip(value, top):
    return jnp.minimum(jnp.maximum(value, 0), top)


class Table:
    def __init__(self, ref, strips, slots, layers):
        self.ref, self.slots, self.layers = ref, slots, layers
        self.count = strips * slots
        self.base = ref.shape[0] - 4 * self.count - strips

    def pick(self, which, home, slot):
        return self.ref[self.base + which * self.count + home * self.slots + slot]

    def column(self, home, slot):
        return self.pick(0, home, slot)

    def shears(self, home, slot):
        angle = self.pick(1, home, slot)
        return [self.ref[angle * self.layers + z] for z in range(self.layers)]

    def slot(self, home, quota):
        found = jnp.int32(0)
        for slot in range(self.slots):
            found = jnp.where(self.pick(2, home, slot) == quota, slot, found)
        return found

    def offset(self, home, slot):
        return self.pick(3, home, slot)

    def alive(self, home, slot):
        return slot < self.ref[self.base + 4 * self.count + home]


def fill_kernel(shear, scan_x, scan_y, slot_angle, owner, counts, table):
    place = 0
    for i in range(shear.shape[0]):
        for z in range(shear.shape[1]):
            table[place] = shear[i, z]
            place += 1
    _, slots, strips = scan_x.shape
    for ref in (scan_y, slot_angle, owner, scan_x):
        for home in range(strips):
            for slot in range(slots):
                table[place] = ref[0, slot, home]
                place += 1
    for home in range(strips):
        table[place] = counts[0, home]
        place += 1


def project_kernel(strips, slots, mine, kinds, *refs):
    strip = lax.axis_index("strip")
    depth = lax.axis_index("depth")
    half = depth if mine else 1 - depth
    table, crystal, *parts = refs
    layers, _, wx, ny = crystal.shape
    ints = Table(table, strips, slots, layers)
    frame = parts[0].shape[-1]
    rows = []
    columns = []
    for kind, out in zip(kinds, parts):
        home = clip(strip - (2 * half if kind == 0 else 1), strips - 1)
        back = wx * (1 - half if kind == 1 else half)
        for quota in range(slots):
            slot = ints.slot(home, quota)
            start = ints.offset(home, slot) - back
            rows.append(
                jnp.concatenate(
                    [
                        band_matrix(out.shape[2], wx, start + shear)
                        for shear in ints.shears(home, slot)
                    ],
                    axis=1,
                )
            )
            columns.append(band_matrix(ny, frame, -ints.column(home, slot)))
    rows = jnp.concatenate(rows, axis=0)
    lifted = [
        dot(rows, jnp.concatenate([crystal[z, part] for z in range(layers)], axis=0)).astype(BF)
        for part in range(2)
    ]
    place = 0
    for entry, out in enumerate(parts):
        tall = out.shape[2]
        for quota in range(slots):
            both = jnp.concatenate([x[place : place + tall] for x in lifted], axis=0)
            band = dot(both, columns[entry * slots + quota]).astype(out.dtype)
            out[quota, 0] = band[:tall]
            out[quota, 1] = band[tall:]
            place += tall


def add_kernel(near, far, out):
    out[...] = (near[...] + far[...].astype(F32)).astype(out.dtype)


def cut_kernel(strips, angles, slots, layers, window, table, picks, alive):
    ints = Table(table, strips, slots, layers)
    quarter = strips // 4
    strip = lax.axis_index("strip")
    plane = lax.axis_index("angle")
    depth = lax.axis_index("depth")
    share = window - MAX_SHEAR
    for quota in range(slots):
        home = lax.rem(strip + (strips - 1) + 4 * (strips - quota % quarter), strips)
        slot = ints.slot(home, quota)
        live = jnp.logical_and(home <= strips - 3, ints.alive(home, slot))
        alive[quota] = jnp.full(alive.shape[1:], jnp.where(live, 1.0, 0.0), F32)
        offset = ints.offset(home, slot)
        for shift in range(angles):
            target = lax.rem(plane + shift, angles)
            for kind in range(2):
                reach = 2 * depth if kind == 0 else 1
                first = reach * (share * angles) + share * target - offset - MAX_SHEAR
                place = (2 * shift + kind) * window
                picks[quota, place : place + window] = band_matrix(window, picks.shape[2], first)


def section_kernel(moved, middle, middle_far, probe, tab, out, waves):
    slots, _, half, frame = moved.shape
    here = pl.ds(pl.multiple_of(lax.axis_index("depth") * half, half), half)
    p_re = probe[0, here].astype(F32)
    p_im = probe[1, here].astype(F32)
    for quota in range(slots):
        w_re, w_im = (
            moved[quota, part].astype(F32)
            + middle[quota, part].astype(F32)
            + middle_far[quota, part].astype(F32)
            for part in range(2)
        )
        to = slice(quota * half, (quota + 1) * half)
        waves[to, :frame] = (p_re * w_re - p_im * w_im).astype(BF)
        waves[to, frame:] = (p_re * w_im + p_im * w_re).astype(BF)
    out[...] = dot(waves[...], tab[0]).astype(BF)


def transform_kernel(angles, slots, window, *refs):
    section_near, section_far, near, far, probe, tab, picks, alive = refs[:8]
    outs = refs[8 : 8 + 2 * angles]
    sections, levels = refs[8 + 2 * angles :]
    depth = lax.axis_index("depth")
    half, frame = near.shape[1:]
    row = pl.multiple_of(depth * half, half)
    row_far = pl.multiple_of((1 - depth) * half, half)
    for quota in range(slots):
        levels[quota, pl.ds(row, half)] = near[quota]
        levels[quota, pl.ds(row_far, half)] = far[quota]

    def side_by_side(x, dtype=BF):
        return jnp.concatenate(
            [
                jnp.concatenate(
                    [
                        x[q * frame : (q + 1) * frame, p * frame : (p + 1) * frame]
                        for q in range(slots)
                    ],
                    axis=1,
                )
                for p in range(2)
            ],
            axis=0,
        ).astype(dtype)

    ahead = tab[0]
    behind = tab[1]
    for first, x in ((row, section_near), (row_far, section_far)):
        for quota in range(slots):
            for part in range(2):
                sections[
                    pl.ds(part * frame + first, half), quota * frame : (quota + 1) * frame
                ] = x[quota * half : (quota + 1) * half, part * frame : (part + 1) * frame]
    section = sections[...]
    spectrum = dot(behind, section)
    p_re = probe[0].astype(F32)
    p_im = probe[1].astype(F32)
    residuals = []
    for quota in range(slots):
        s_re = spectrum[:frame, quota * frame : (quota + 1) * frame]
        s_im = spectrum[frame:, quota * frame : (quota + 1) * frame]
        inverse_size = jnp.minimum(lax.rsqrt(s_re * s_re + s_im * s_im), 1.0)
        factor = (1.0 - levels[quota].astype(F32) * inverse_size) * alive[quota, :1, :1]
        residuals.append(jnp.concatenate([s_re * factor, s_im * factor], axis=1).astype(BF))
    inverse = side_by_side(dot(jnp.concatenate(residuals, axis=0), behind))
    wave = dot(ahead, inverse)
    for quota in range(slots):
        b_re = wave[:frame, quota * frame : (quota + 1) * frame]
        b_im = wave[frame:, quota * frame : (quota + 1) * frame]
        back = jnp.concatenate(
            [p_re * b_re + p_im * b_im, p_re * b_im - p_im * b_re], axis=1
        ).astype(BF)
        cut = dot(picks[quota], back).astype(BF)
        for place, out in enumerate(outs):
            rows = cut[place * window : (place + 1) * window]
            held = out.shape[0]
            if held == slots:
                out[quota, 0] = rows[:, :frame]
                out[quota, 1] = rows[:, frame:]
                continue

            @pl.when(depth == quota // held)
            def _():
                out[quota % held, 0] = rows[:, :frame]
                out[quota % held, 1] = rows[:, frame:]


def place_kernel(strips, slots, share, rounds, laps, *refs):
    tables, refs = refs[:laps], refs[laps:]
    strip = lax.axis_index("strip")
    depth = lax.axis_index("depth")
    for (items, layers), left, columns in zip(rounds, refs[::2], refs[1::2]):
        _, frame, ny = columns.shape
        window = left.shape[1] // columns.shape[0]
        entry = 0
        for lap, kind, held in items:
            ints = Table(tables[lap], strips, slots, layers)
            reach = (2 * depth, 2 - 2 * depth, 1, 1)[kind]
            home = clip(strip - reach, strips - 1)
            for place in range(held):
                quota = place
                if held < slots:
                    quota = place + held * (depth if kind == 2 else 1 - depth)
                slot = ints.slot(home, quota)
                for z, shear in enumerate(ints.shears(home, slot)):
                    left[z * share : (z + 1) * share, entry * window : (entry + 1) * window] = (
                        band_matrix(share, window, MAX_SHEAR - shear)
                    )
                columns[entry] = band_matrix(frame, ny, ints.column(home, slot))
                entry += 1


def deposit_kernel(before, last, scale, left, columns, *refs):
    refs, total, sems = (refs[:-2], *refs[-2:]) if last else (refs, refs[-1], None)
    refs, out = refs[:-1], refs[-1]
    blocks, sums = (refs[:-1], refs[-1]) if before else (refs, None)
    layers, _, share, ny = out.shape
    window = blocks[0].shape[2]
    values = ([], [])
    entry = 0
    for block in blocks:
        for place in range(block.shape[0]):
            both = jnp.concatenate([block[place, 0], block[place, 1]], axis=0)
            placed = dot(both, columns[entry]).astype(BF)
            values[0].append(placed[:window])
            values[1].append(placed[window:])
            entry += 1
    left = left[...]
    copies = []
    for part in range(2):
        grown = dot(left, jnp.concatenate(values[part], axis=0))
        for z in range(layers):
            piece = grown[z * share : (z + 1) * share]
            if before:
                piece = piece + sums[z, part]
            total[z, part] = piece * scale if last else piece
            if last:
                copies.append(
                    pltpu.make_async_copy(total.at[z, part], out.at[z, part], sems.at[z, part])
                )
                copies[-1].start()
    for copy in copies:
        copy.wait()


def body(mesh_shape, crystal, probe, amplitude, shear, scan_x, scan_y, slot_angle, owner_slot, counts):
    strips, angles, depths = (mesh_shape[n] for n in ("strip", "angle", "depth"))
    slots = owner_slot.shape[2]
    quarter = strips // 4
    lanes = slots // quarter
    layers, _, wx, ny = crystal.shape
    frame = probe.shape[-1]
    share = wx // angles
    window = share + MAX_SHEAR
    half = amplitude.shape[1]
    axes = ("strip", "angle", "depth")
    params = pltpu.CompilerParams(vmem_limit_bytes=VMEM_BYTES)
    smem = pl.BlockSpec(memory_space=pltpu.SMEM)
    vmem = pl.BlockSpec(memory_space=pltpu.VMEM)

    def cost(micros):
        return pl.CostEstimate(flops=int(micros * 8e8), bytes_accessed=0, transcendentals=0)

    def swap(x):
        return lax.ppermute(x, "depth", [(d, (d + 1) % depths) for d in range(depths)])

    def permute(x, move):
        pairs = []
        for s in range(strips):
            for a in range(angles):
                for d in range(depths):
                    to = move(s, a, d)
                    if to is not None:
                        pairs.append(
                            (
                                (s * angles + a) * depths + d,
                                (to[0] * angles + to[1]) * depths + to[2],
                            )
                        )
        return lax.ppermute(x, axes, pairs)

    def ring(x, turn, lap):
        def move(s, a, d):
            way = turn if d == 0 else -turn
            if 0 <= s + way < strips:
                return s + way, (a + lap) % angles, d
            return s, a, 1 - d

        return permute(x, move)

    def far(x, way, lap, hops, forward):
        def move(s, a, d):
            reach = 2 * d if way else 1
            home = s - reach if forward else (s - 1 - 4 * hops) % strips
            if not 0 <= home <= strips - 3:
                return None
            to = (home + 1 + 4 * hops) % strips if forward else home + reach
            return to, (a + lap) % angles, d

        return permute(x, move)

    amplitude_far = swap(amplitude)
    by_slot = [jnp.swapaxes(x, 1, 2) for x in (scan_x, scan_y, slot_angle, owner_slot)]
    sources = (shear, *by_slot, counts)
    entries = shear.shape[0] * layers + 4 * strips * slots + strips
    table = pl.pallas_call(
        fill_kernel,
        out_shape=jax.ShapeDtypeStruct((entries,), jnp.int32),
        in_specs=[smem] * 6,
        out_specs=smem,
        compiler_params=pltpu.CompilerParams(vmem_limit_bytes=FILL_VMEM_BYTES),
        cost_estimate=cost(3),
        name="fill",
    )(*sources)
    sent = pl.pallas_call(
        functools.partial(project_kernel, strips, slots, False, (0,)),
        out_shape=jax.ShapeDtypeStruct((slots, 2, half, frame), BF),
        in_specs=[smem, vmem],
        out_specs=vmem,
        compiler_params=params,
        cost_estimate=cost(1.5),
        name="project_far",
    )(table, crystal)
    arrived = swap(sent)

    def project(kinds, dtype, micros, name):
        return pl.pallas_call(
            functools.partial(project_kernel, strips, slots, True, kinds),
            out_shape=[jax.ShapeDtypeStruct((slots, 2, half, frame), dtype)] * len(kinds),
            in_specs=[smem, vmem],
            out_specs=[vmem] * len(kinds),
            compiler_params=params,
            cost_estimate=cost(micros),
            name=name,
        )

    (moving,) = project((0,), F32, 1.5, "project_near")(table, crystal)
    moving = pl.pallas_call(
        add_kernel,
        out_shape=jax.ShapeDtypeStruct(moving.shape, BF),
        in_specs=[vmem] * 2,
        out_specs=vmem,
        compiler_params=params,
        cost_estimate=cost(0.5),
        name="add",
    )(moving, arrived)

    moving, middle_table = lax.optimization_barrier((moving, table))
    middle, middle_sent = project((1, 2), BF, 1.5, "project_middle")(middle_table, crystal)

    def by_hops(x, near, beyond):
        if quarter == 1:
            return near(x)
        pieces = []
        for hops in range(quarter):
            piece = x[hops::quarter]
            pieces.append(near(piece) if hops == 0 else beyond(piece, hops))
        return jnp.stack(pieces, axis=1).reshape(x.shape)

    moved = by_hops(moving, lambda x: ring(x, 1, 0), lambda x, n: far(x, 1, 0, n, True))
    middle, middle_sent = (
        by_hops(x, lambda x: x, lambda x, n: far(x, 0, 0, n, True)) for x in (middle, middle_sent)
    )
    middle_far = swap(middle_sent)
    picks, alive = pl.pallas_call(
        functools.partial(cut_kernel, strips, angles, slots, layers, window),
        out_shape=[
            jax.ShapeDtypeStruct((slots, 2 * angles * window, frame), BF),
            jax.ShapeDtypeStruct((slots, 8, 128), F32),
        ],
        in_specs=[smem],
        out_specs=[vmem] * 2,
        compiler_params=params,
        cost_estimate=cost(0.5),
        name="cut",
    )(middle_table)
    moved, amplitude_far, picks, alive, table = lax.optimization_barrier(
        (moved, amplitude_far, picks, alive, middle_table)
    )
    tables = [table] + [
        lax.ppermute(table, "angle", [(a, (a + t) % angles) for a in range(angles)])
        for t in range(1, angles)
    ]
    tab = jnp.asarray(dft_tables(frame))
    section_near = pl.pallas_call(
        section_kernel,
        out_shape=jax.ShapeDtypeStruct((slots * half, 2 * frame), BF),
        in_specs=[vmem] * 5,
        out_specs=vmem,
        scratch_shapes=[pltpu.VMEM((slots * half, 2 * frame), BF)],
        compiler_params=params,
        cost_estimate=cost(0.7),
        name="section",
    )(moved, middle, middle_far, probe, tab)
    split = quarter == 1 and slots % depths == 0
    held = slots // depths if split else slots
    cuts = pl.pallas_call(
        functools.partial(transform_kernel, angles, slots, window),
        out_shape=[
            jax.ShapeDtypeStruct((held if i > 1 and i % 2 else slots, 2, window, frame), BF)
            for i in range(2 * angles)
        ],
        in_specs=[vmem] * 8,
        out_specs=[vmem] * (2 * angles),
        scratch_shapes=[
            pltpu.VMEM((2 * frame, slots * frame), BF),
            pltpu.VMEM((slots, frame, frame), BF),
        ],
        compiler_params=params,
        cost_estimate=cost(3),
        name="transform",
    )(
        section_near, swap(section_near),
        amplitude, amplitude_far, probe, tab,
        picks, alive,
    )
    blocks = {}
    for lap in reversed(range(angles)):
        blocks[lap, 0] = by_hops(
            cuts[2 * lap],
            lambda x: ring(x, -1, lap),
            lambda x, n: far(x, 1, lap, n, False),
        )
        blocks[lap, 2] = by_hops(
            cuts[2 * lap + 1],
            lambda x: x
            if lap == 0
            else lax.ppermute(x, "angle", [(a, (a + lap) % angles) for a in range(angles)]),
            lambda x, n: far(x, 0, lap, n, False),
        )
    scale = 1.0 / (shear.shape[0] * angles)

    later = range(1, angles)
    keys = [(lap, kind) for lap in later for kind in (0, 2)] + [(0, 0)]
    shared = {0: 1, 2: 3} if split else {0: 1}
    rounds = [
        [(lap, kind, blocks[lap, kind].shape[0]) for lap, kind in keys + [(0, 2)]],
        [(lap, shared[kind], blocks[lap, kind].shape[0]) for lap, kind in keys if kind in shared],
    ]
    shapes = []
    for items in rounds:
        entries = sum(held for _, _, held in items)
        shapes.append(jax.ShapeDtypeStruct((layers * share, entries * window), BF))
        shapes.append(jax.ShapeDtypeStruct((entries, frame, ny), BF))
    places = pl.pallas_call(
        functools.partial(
            place_kernel, strips, slots, share, [(items, layers) for items in rounds], angles
        ),
        out_shape=shapes,
        in_specs=[smem] * angles,
        out_specs=[vmem] * len(shapes),
        compiler_params=params,
        cost_estimate=cost(0.05),
        name="place",
    )(*tables)
    arrivals = lax.optimization_barrier([blocks[key] for key in keys] + list(places))
    blocks.update(zip(keys, arrivals))
    places = arrivals[len(keys) :]
    others = [(lap, shared[kind]) for lap, kind in keys if kind in shared]
    own = keys + [(0, 2)]
    blocks.update({(lap, shared[kind]): swap(blocks[lap, kind]) for lap, kind in keys if kind in shared})

    def deposit(items, places, sums, last):
        sums = [] if sums is None else [sums]
        shape = (layers, 2, share, ny)
        return pl.pallas_call(
            functools.partial(deposit_kernel, bool(sums), last, scale),
            out_shape=jax.ShapeDtypeStruct(shape, F32),
            in_specs=[vmem] * (2 + len(items) + len(sums)),
            out_specs=pl.BlockSpec(memory_space=pltpu.HBM) if last else vmem,
            scratch_shapes=[pltpu.VMEM(shape, F32), pltpu.SemaphoreType.DMA((layers, 2))]
            if last
            else [],
            compiler_params=params,
            cost_estimate=cost(0.05),
            name="deposit",
        )(*places, *(blocks[item] for item in items), *sums)

    return deposit(others, places[2:], deposit(own, places[:2], None, False), True)


def solution(mesh):
    placed = (
        P(("groups", "depth"), None, "strip", None),
        P(),
        P("angle", ("groups", "strip", "depth"), None),
        P(("groups", "angle"), "depth"),
        P(("groups", "angle"), None, None),
        P(("groups", "angle"), None, None),
        P(("groups", "angle"), None, None),
        P(("groups", "angle"), None, None),
        P(("groups", "angle"), None),
    )
    return jax.shard_map(
        functools.partial(body, dict(mesh.shape)),
        mesh=mesh,
        in_specs=placed,
        out_specs=P(("groups", "depth"), None, ("strip", "angle"), None),
        check_vma=False,
    )
```
